256 devices in a mesh: row: 32 (over y, x, core), col: 8 (over z).
Axes of the slice: x: 4, y: 4, z: 8, core: 2. Of those that a mesh axis runs over, the one named last changes fastest.
Arguments:
- tiles: bfloat16 [32, 8, 48, 256, 256], P('row', 'col'), may hold values from -6 to 6
- coords: int32 [32, 8, 48, 2], P('row', 'col'), may hold values from 0 to 7, as said below
- counts: int32 [32, 8], P('row', 'col'), may hold values from 8 to 48, as said below
- panel: bfloat16 [65536, 512], P(('row', 'col')), may hold values from -6 to 6
Outputs:
- basis: float32 [16384, 512], P(('col', 'row'))
The draws below stay inside these ranges and needn't reach their ends.
Inputs may be any that keep to these rules, and one draw needn't show every extreme that they name: `coords`: on each device the first counts slots name distinct positions, block row below 8 and block column below 8; later slots name valid positions too. `counts`: some device holds 48 live tiles in every draw.
All inputs are finite; a program needn't handle non-finite values.
Results may differ from the reference program's by a relative error of at most 0.0003.
Values may be sent and summed in bfloat16 or wider, within the bound.
A program may use at most 128 MiB of HBM per device.

```python
import jax
import jax.numpy as jnp
from jax import lax

TILE = 256
K = 512
RB_DEV = 8
CB_DEV = 8
TILES_DEV = 48
ROWS = 65536
COLS = 16384
N_ROW = 32
N_COL = 8


def draw_coords(key, part):
    key = jax.random.fold_in(key, 1)
    keys = jax.random.split(key, N_ROW * N_COL)
    perms = jax.vmap(lambda k: jax.random.permutation(k, RB_DEV * CB_DEV))(keys)[:, :TILES_DEV]
    perms = perms.astype(jnp.int32)
    pairs = jnp.stack([perms // CB_DEV, perms % CB_DEV], axis=-1)
    return pairs.reshape(N_ROW, N_COL, TILES_DEV, 2).astype(jnp.int32)


def draw_counts(key, part):
    key = jax.random.fold_in(key, 2)
    first, second = jax.random.split(key)
    lowest = TILES_DEV // 6
    spread = TILES_DEV - lowest
    draws = jax.random.randint(first, (N_ROW * N_COL,), 0, spread + 1).astype(jnp.int32)
    loads = lowest + draws * draws // spread
    busiest = jax.random.randint(second, (), 0, N_ROW * N_COL).astype(jnp.int32)
    loads = jnp.where(jnp.arange(N_ROW * N_COL, dtype=jnp.int32) == busiest, TILES_DEV, loads)
    return loads.reshape(N_ROW, N_COL).astype(jnp.int32)


def steps_of(own_key, shape, cuts, smallest, largest):
    def one(position, shards_of):
        steps = jax.random.uniform(jax.random.fold_in(jax.random.fold_in(own_key, 6), position), (shards_of,), jnp.float32, smallest / len(cuts), largest / len(cuts))
        return jnp.repeat(jnp.exp(steps), shape[position] // shards_of).reshape((-1,) + (1,) * (len(shape) - position - 1))

    gain = one(*cuts[0])
    for cut in cuts[1:]:
        gain = gain * one(*cut)
    return gain


def gaussian(own_key, extent, width, most, cuts=(), kind=jnp.bfloat16):
    factor_of = steps_of(own_key, extent, cuts, -0.22, 0.18) if cuts else 1.0
    entries = jax.random.normal(own_key, extent, jnp.float32) * width * factor_of
    return jnp.minimum(jnp.maximum(entries, -most), most).astype(kind)


def setup_inputs(seed: int = 0) -> dict:
    key_list = jax.random.split(jax.random.key(seed), 5)
    tiles = gaussian(key_list[0], (N_ROW, N_COL, TILES_DEV, TILE, TILE), 1.0, 6.0, ((0, 32), (1, 8)))
    coords = draw_coords(jax.random.fold_in(key_list[4], 71), 0)
    counts = draw_counts(jax.random.fold_in(key_list[4], 71), 0)
    panel = gaussian(key_list[3], (ROWS, K), 1.0, 6.0, ((0, 256),))
    return dict(tiles=tiles, coords=coords, counts=counts, panel=panel)


def reference(tiles, coords, counts, panel):
    hi = lax.Precision.HIGHEST
    blocks = panel.reshape(N_ROW, RB_DEV, TILE, K)
    slots = jnp.arange(TILES_DEV, dtype=jnp.int32)

    def add_device(index, total):
        rpos = index // N_COL
        cpos = index % N_COL
        values = tiles[rpos, cpos].astype(jnp.float32)
        where = coords[rpos, cpos]
        live = (slots < counts[rpos, cpos]).astype(jnp.float32)
        pick = (where[:, 0][:, None] == jnp.arange(RB_DEV, dtype=jnp.int32)[None, :]).astype(jnp.float32)
        chosen = jnp.einsum('sb,btk->stk', pick, blocks[rpos].astype(jnp.float32), precision=hi)
        prods = jnp.einsum('sij,sik->sjk', values, chosen, precision=hi)
        place = (where[:, 1][:, None] == jnp.arange(CB_DEV, dtype=jnp.int32)[None, :]).astype(jnp.float32) * live[:, None]
        part = jnp.einsum('sb,sjk->bjk', place, prods, precision=hi)
        return total.at[cpos].add(part)
    start = jnp.zeros((N_COL, CB_DEV, TILE, K), jnp.float32)
    product = lax.fori_loop(0, N_ROW * N_COL, add_device, start).reshape(COLS, K)
    gram = jnp.dot(product.T, product, precision=hi)
    lower = jnp.linalg.cholesky(gram)
    solved = jax.scipy.linalg.solve_triangular(lower, product.T, lower=True)
    return (solved.T * jnp.sqrt(jnp.float32(COLS))).astype(jnp.float32)
```

```python
import jax
import jax.numpy as jnp
from jax import lax
from jax.experimental import pallas as pl
from jax.experimental.pallas import tpu as pltpu
from jax.sharding import PartitionSpec as P

F32 = jnp.float32
BF16 = jnp.bfloat16
HI = lax.Precision.HIGHEST
TILE = 256
NB = 8
K = 512
SLOTS = 48
VMEM = pltpu.VMEM
SMEM = pltpu.SMEM


def mm(a, b, dims):
    return lax.dot_general(a, b, (dims, ((), ())), precision=HI, preferred_element_type=F32)


def tile_kernel(slot_ref, tiles_hbm, panel_ref, out_ref, tiles_ref, at_ref, sem):
    copy = pltpu.make_async_copy(tiles_hbm, tiles_ref, sem)
    copy.start()
    copy.wait()

    def build(pos, carry):
        slot = slot_ref[pos]
        tile = tiles_ref[jnp.minimum(slot, SLOTS - 1)]
        tile = jnp.where(slot < SLOTS, tile.astype(F32), 0.0).T.astype(BF16)
        block_row, block_col = pos // NB, pos % NB
        at_ref[block_row, pl.ds(pl.multiple_of(block_col * TILE, TILE), TILE), :] = tile
        return carry

    lax.fori_loop(0, NB * NB, build, 0)

    def multiply(col, carry):
        rows = pl.ds(pl.multiple_of(col * TILE, TILE), TILE)
        total = jnp.zeros((TILE, K), F32)
        for b in range(NB):
            total += jnp.dot(
                at_ref[b, rows, :],
                panel_ref[b * TILE:(b + 1) * TILE, :],
                preferred_element_type=F32,
            )
        out_ref[rows, :] = total
        return carry

    lax.fori_loop(0, NB, multiply, 0)


def tile_product(slot_of, tiles, panel):
    return pl.pallas_call(
        tile_kernel,
        out_shape=jax.ShapeDtypeStruct((NB * TILE, K), F32),
        in_specs=[
            pl.BlockSpec(memory_space=SMEM),
            pl.BlockSpec(memory_space=pl.ANY),
            pl.BlockSpec(memory_space=VMEM),
        ],
        out_specs=pl.BlockSpec(memory_space=VMEM),
        scratch_shapes=[
            VMEM((SLOTS, TILE, TILE), BF16),
            VMEM((NB, NB * TILE, TILE), BF16),
            pltpu.SemaphoreType.DMA,
        ],
        compiler_params=pltpu.CompilerParams(vmem_limit_bytes=40 * 2**20),
        name="tile_product",
    )(slot_of, tiles, panel)


def factor(w_ref, b):
    n = 128
    sub = lax.broadcasted_iota(jnp.int32, (b, 128), 0)
    for c0 in range(0, n, b):
        left = w_ref[c0:c0 + b, :128]
        right = w_ref[c0:c0 + b, 128:]
        cols = [jnp.broadcast_to(left[:, c0 + j:c0 + j + 1], (b, 128)) for j in range(b)]
        pivots = jnp.ones((b, 128), F32)
        for j in range(b):
            pivot = cols[j][j:j + 1, :]
            f = jnp.where(sub > j, cols[j] * (1.0 / pivot), 0.0)
            for m in range(j + 1, b):
                cols[m] = cols[m] - f * cols[m][j:j + 1, :]
            if j < b - 1:
                left = left - f * left[j:j + 1, :]
                right = right - f * right[j:j + 1, :]
            pivots = jnp.where(sub == j, pivot, pivots)
        norm = lax.rsqrt(pivots)
        left = left * norm
        right = right * norm
        w_ref[c0:c0 + b, :128] = left
        w_ref[c0:c0 + b, 128:] = right
        e = c0 + b
        if e < n:
            both = jnp.concatenate([left, right], axis=1)
            t = mm(left, both, ((0,), (0,)))
            w_ref[e:, :] = w_ref[e:, :] - t[e:, :]


def basis_kernel(scale, gram_ref, rows_ref, out_ref, s_ref, w_ref):
    eye = (
        lax.broadcasted_iota(jnp.int32, (128, 128), 0)
        == lax.broadcasted_iota(jnp.int32, (128, 128), 1)
    ).astype(F32)
    s_ref[...] = gram_ref[...]
    out_ref[...] = rows_ref[...]
    for i in range(K // 128):
        lo, hi = i * 128, (i + 1) * 128
        w_ref[:, :128] = s_ref[lo:hi, lo:hi]
        w_ref[:, 128:] = eye
        factor(w_ref, 16)
        inv = w_ref[:, 128:]
        x = mm(out_ref[:, lo:hi], inv, ((1,), (1,)))
        out_ref[:, lo:hi] = x * scale
        if hi < K:
            u = mm(inv, s_ref[lo:hi, hi:], ((1,), (0,)))
            s_ref[hi:, hi:] = s_ref[hi:, hi:] - mm(u, u, ((0,), (0,)))
            out_ref[:, hi:] = out_ref[:, hi:] - mm(x, u, ((1,), (0,)))


def cholesky_basis(gram, rows, scale):
    return pl.pallas_call(
        lambda *refs: basis_kernel(scale, *refs),
        out_shape=jax.ShapeDtypeStruct(rows.shape, F32),
        in_specs=[pl.BlockSpec(memory_space=VMEM)] * 2,
        out_specs=pl.BlockSpec(memory_space=VMEM),
        scratch_shapes=[VMEM((K, K), F32), VMEM((128, 256), F32)],
        compiler_params=pltpu.CompilerParams(vmem_limit_bytes=40 * 2**20),
        name="cholesky_basis",
    )(gram, rows)


def local(tiles, coords, counts, panel):
    where = coords[0, 0]
    position = where[:, 0] * NB + where[:, 1]
    slots = jnp.arange(SLOTS, dtype=jnp.int32)
    live = slots < counts[0, 0]
    match = (position[None, :] == jnp.arange(NB * NB, dtype=jnp.int32)[:, None]) & live[None, :]
    slot_of = jnp.min(jnp.where(match, slots[None, :], SLOTS), axis=1)

    gathered = lax.all_gather(panel, "col", axis=0, tiled=True)
    partial_sum = tile_product(slot_of, tiles[0, 0], gathered)
    own_rows = lax.psum_scatter(partial_sum, "row", scatter_dimension=0, tiled=True)
    local_gram = mm(own_rows, own_rows, ((0,), (0,)))
    gram = lax.psum(local_gram, ("row", "col"))
    scale = float((partial_sum.shape[0] * 8) ** 0.5)
    return cholesky_basis(gram, own_rows, scale)


def solution(mesh):
    placed = (
        P("row", "col", None, None, None),
        P("row", "col", None, None),
        P("row", "col"),
        P(("row", "col"), None),
    )
    return jax.shard_map(
        local, mesh=mesh, in_specs=placed, out_specs=P(("col", "row"), None), check_vma=False
    )
```

```python
import jax
import jax.numpy as jnp
from jax import lax
from jax.experimental import pallas as pl
from jax.experimental.pallas import tpu as pltpu
from jax.sharding import PartitionSpec as P

F32 = jnp.float32
BF16 = jnp.bfloat16
HI = lax.Precision.HIGHEST
TILE = 256
NB = 8
K = 512
SLOTS = 48
VMEM = pltpu.VMEM
SMEM = pltpu.SMEM
MESH = pl.DeviceIdType.MESH

CHIPS = 16
DEPTH = 8
BLOCKS = [(i, j) for i in range(4) for j in range(i, 4)]
WHERE = {ij: n * 128 for n, ij in enumerate(BLOCKS)}
HALF = 640
PIECE = 40


def mm(a, b, dims):
    return lax.dot_general(a, b, (dims, ((), ())), precision=HI, preferred_element_type=F32)


def tile_kernel(slot_ref, tiles_hbm, panel_ref, out_ref, tiles_ref, at_ref, sem):
    copy = pltpu.make_async_copy(tiles_hbm, tiles_ref, sem)
    copy.start()
    copy.wait()

    def build(pos, carry):
        slot = slot_ref[pos]
        tile = tiles_ref[jnp.minimum(slot, SLOTS - 1)]
        tile = jnp.where(slot < SLOTS, tile.astype(F32), 0.0).T.astype(BF16)
        block_row, block_col = pos // NB, pos % NB
        at_ref[block_row, pl.ds(pl.multiple_of(block_col * TILE, TILE), TILE), :] = tile
        return carry

    lax.fori_loop(0, NB * NB, build, 0)

    def multiply(col, carry):
        rows = pl.ds(pl.multiple_of(col * TILE, TILE), TILE)
        total = jnp.zeros((TILE, K), F32)
        for b in range(NB):
            total += jnp.dot(
                at_ref[b, rows, :],
                panel_ref[b * TILE:(b + 1) * TILE, :],
                preferred_element_type=F32,
            )
        out_ref[rows, :] = total
        return carry

    lax.fori_loop(0, NB, multiply, 0)


def tile_product(slot_of, tiles, panel):
    return pl.pallas_call(
        tile_kernel,
        out_shape=jax.ShapeDtypeStruct((NB * TILE, K), F32),
        in_specs=[
            pl.BlockSpec(memory_space=SMEM),
            pl.BlockSpec(memory_space=pl.ANY),
            pl.BlockSpec(memory_space=VMEM),
        ],
        out_specs=pl.BlockSpec(memory_space=VMEM),
        scratch_shapes=[
            VMEM((SLOTS, TILE, TILE), BF16),
            VMEM((NB, NB * TILE, TILE), BF16),
            pltpu.SemaphoreType.DMA,
        ],
        compiler_params=pltpu.CompilerParams(vmem_limit_bytes=40 * 2**20),
        name="tile_product",
    )(slot_of, tiles, panel)


def factor(w_ref, b):
    n = 128
    sub = lax.broadcasted_iota(jnp.int32, (b, 128), 0)
    for c0 in range(0, n, b):
        left = w_ref[c0:c0 + b, :128]
        right = w_ref[c0:c0 + b, 128:]
        cols = [jnp.broadcast_to(left[:, c0 + j:c0 + j + 1], (b, 128)) for j in range(b)]
        pivots = jnp.ones((b, 128), F32)
        for j in range(b):
            pivot = cols[j][j:j + 1, :]
            f = jnp.where(sub > j, cols[j] * (1.0 / pivot), 0.0)
            for m in range(j + 1, b):
                cols[m] = cols[m] - f * cols[m][j:j + 1, :]
            if j < b - 1:
                left = left - f * left[j:j + 1, :]
                right = right - f * right[j:j + 1, :]
            pivots = jnp.where(sub == j, pivot, pivots)
        norm = lax.rsqrt(pivots)
        left = left * norm
        right = right * norm
        w_ref[c0:c0 + b, :128] = left
        w_ref[c0:c0 + b, 128:] = right
        e = c0 + b
        if e < n:
            both = jnp.concatenate([left, right], axis=1)
            t = mm(left, both, ((0,), (0,)))
            w_ref[e:, :] = w_ref[e:, :] - t[e:, :]


def gram_kernel(scale, rows_ref, out_ref, mine, twin, parts, planes, gram, x_ref, s_ref, w_ref,
                pair_send, pair_recv, part_send, part_recv, plane_send, plane_recv, gather_send, gather_recv):
    row, z = lax.axis_index("row"), lax.axis_index("col")
    chip, core = row // 2, row % 2
    other = 1 - core

    def at_chip(i):
        return (lax.rem(chip + i, CHIPS) * 2 + core, z)

    def at_plane(i):
        return (row, lax.rem(z + i, DEPTH))

    twin_id = (chip * 2 + other, z)
    barrier = pltpu.get_barrier_semaphore()

    def hello_chip(i, c):
        pl.semaphore_signal(barrier, inc=1, device_id=at_chip(i), device_id_type=MESH)
        return c

    def hello_plane(i, c):
        pl.semaphore_signal(barrier, inc=1, device_id=at_plane(i), device_id_type=MESH)
        return c

    pl.semaphore_signal(barrier, inc=1, device_id=twin_id, device_id_type=MESH)
    lax.fori_loop(1, CHIPS, hello_chip, 0)
    lax.fori_loop(1, DEPTH, hello_plane, 0)

    for i in range(4):
        g = mm(rows_ref[:, i * 128:(i + 1) * 128], rows_ref[:, i * 128:], ((0,), (0,)))
        for j in range(i, 4):
            at = WHERE[i, j]
            mine[at:at + 128, :] = g[:, (j - i) * 128:(j - i + 1) * 128]
    pl.semaphore_wait(barrier, 1 + CHIPS - 1 + DEPTH - 1)

    copy = pltpu.make_async_remote_copy(
        src_ref=mine.at[pl.ds(pl.multiple_of(other * HALF, 8), HALF)], dst_ref=twin,
        send_sem=pair_send.at[0], recv_sem=pair_recv.at[0], device_id=twin_id, device_id_type=MESH)
    copy.start()
    copy.wait()
    own = pl.ds(pl.multiple_of(core * HALF, 8), HALF)
    twin[...] = twin[...] + mine[own, :]

    def part(i):
        there = lax.rem(chip + i, CHIPS)
        return pltpu.make_async_remote_copy(
            src_ref=twin.at[pl.ds(pl.multiple_of(there * PIECE, 8), PIECE)], dst_ref=parts.at[i],
            send_sem=part_send.at[i], recv_sem=part_recv.at[i], device_id=at_chip(i), device_id_type=MESH)

    def start_part(i, c):
        part(i).start()
        return c

    lax.fori_loop(1, CHIPS, start_part, 0)

    def add_part(i, total):
        part(i).wait()
        return total + parts[i]

    total = lax.fori_loop(1, CHIPS, add_part, twin[pl.ds(pl.multiple_of(chip * PIECE, 8), PIECE), :])

    planes[z] = total

    def plane(i):
        return pltpu.make_async_remote_copy(
            src_ref=planes.at[z], dst_ref=planes.at[z],
            send_sem=plane_send.at[i], recv_sem=plane_recv.at[i], device_id=at_plane(i), device_id_type=MESH)

    def start_plane(i, c):
        plane(i).start()
        return c

    def wait_plane(i, c):
        plane(i).wait_send()
        came = lax.rem(z + DEPTH - i, DEPTH)
        pltpu.make_async_remote_copy(
            src_ref=planes.at[came], dst_ref=planes.at[came],
            send_sem=plane_send.at[i], recv_sem=plane_recv.at[i], device_id=at_plane(i), device_id_type=MESH).wait_recv()
        return c

    lax.fori_loop(1, DEPTH, start_plane, 0)
    lax.fori_loop(1, DEPTH, wait_plane, 0)
    total = planes[0]
    for i in range(1, DEPTH):
        total = total + planes[i]

    def slot(n):
        return pl.ds(pl.multiple_of(core * HALF + n * PIECE, 8), PIECE)

    gram[slot(chip), :] = total

    def start_gather(i, c):
        pltpu.make_async_remote_copy(
            src_ref=gram.at[slot(chip)], dst_ref=gram.at[slot(chip)],
            send_sem=gather_send.at[i], recv_sem=gather_recv.at[i], device_id=at_chip(i), device_id_type=MESH).start()
        return c

    def wait_gather(i, c):
        came = lax.rem(chip + CHIPS - i, CHIPS)
        pltpu.make_async_remote_copy(
            src_ref=gram.at[slot(came)], dst_ref=gram.at[slot(came)],
            send_sem=gather_send.at[i], recv_sem=gather_recv.at[i], device_id=at_chip(i), device_id_type=MESH).wait()
        return c

    lax.fori_loop(1, CHIPS, start_gather, 0)
    lax.fori_loop(1, CHIPS, wait_gather, 0)
    there = pl.ds(pl.multiple_of(other * HALF, 8), HALF)
    copy = pltpu.make_async_remote_copy(
        src_ref=gram.at[own], dst_ref=gram.at[own],
        send_sem=pair_send.at[1], recv_sem=pair_recv.at[1], device_id=twin_id, device_id_type=MESH)
    copy.start()
    copy.wait_send()
    pltpu.make_async_remote_copy(
        src_ref=gram.at[there], dst_ref=gram.at[there],
        send_sem=pair_send.at[1], recv_sem=pair_recv.at[1], device_id=twin_id, device_id_type=MESH).wait_recv()

    eye = (
        lax.broadcasted_iota(jnp.int32, (128, 128), 0)
        == lax.broadcasted_iota(jnp.int32, (128, 128), 1)
    ).astype(F32)
    for i, j in BLOCKS:
        at = WHERE[i, j]
        s_ref[i * 128:(i + 1) * 128, j * 128:(j + 1) * 128] = gram[at:at + 128, :]
    x_ref[...] = rows_ref[...]
    for i in range(4):
        lo, hi = i * 128, (i + 1) * 128
        w_ref[:, :128] = s_ref[lo:hi, lo:hi]
        w_ref[:, 128:] = eye
        factor(w_ref, 16)
        inv = w_ref[:, 128:]
        x = mm(x_ref[:, lo:hi], inv, ((1,), (1,)))
        out_ref[:, lo:hi] = x * scale
        if hi < K:
            u = mm(inv, s_ref[lo:hi, hi:], ((1,), (0,)))
            for j in range(i + 1, 4):
                a, b = j * 128, (j + 1) * 128
                s_ref[a:b, a:] = s_ref[a:b, a:] - mm(u[:, a - hi:b - hi], u[:, a - hi:], ((0,), (0,)))
            x_ref[:, hi:] = x_ref[:, hi:] - mm(x, u, ((1,), (0,)))


def gram_basis(rows, scale):
    dma = pltpu.SemaphoreType.DMA
    return pl.pallas_call(
        lambda *refs: gram_kernel(scale, *refs),
        out_shape=jax.ShapeDtypeStruct(rows.shape, F32),
        in_specs=[pl.BlockSpec(memory_space=VMEM)],
        out_specs=pl.BlockSpec(memory_space=VMEM),
        scratch_shapes=[
            VMEM((2 * HALF, 128), F32), VMEM((HALF, 128), F32), VMEM((CHIPS, PIECE, 128), F32),
            VMEM((DEPTH, PIECE, 128), F32), VMEM((2 * HALF, 128), F32), VMEM((64, K), F32),
            VMEM((K, K), F32), VMEM((128, 256), F32),
            dma((2,)), dma((2,)), dma((CHIPS,)), dma((CHIPS,)), dma((DEPTH,)), dma((DEPTH,)), dma((CHIPS,)), dma((CHIPS,)),
        ],
        compiler_params=pltpu.CompilerParams(
            vmem_limit_bytes=40 * 2**20, collective_id=1, has_side_effects=True),
        name="gram_basis",
    )(rows)


def local(tiles, coords, counts, panel):
    where = coords[0, 0]
    position = where[:, 0] * NB + where[:, 1]
    slots = jnp.arange(SLOTS, dtype=jnp.int32)
    live = slots < counts[0, 0]
    match = (position[None, :] == jnp.arange(NB * NB, dtype=jnp.int32)[:, None]) & live[None, :]
    slot_of = jnp.min(jnp.where(match, slots[None, :], SLOTS), axis=1)

    gathered = lax.all_gather(panel, "col", axis=0, tiled=True)
    partial_sum = tile_product(slot_of, tiles[0, 0], gathered)
    own_rows = lax.psum_scatter(partial_sum, "row", scatter_dimension=0, tiled=True)
    scale = float((partial_sum.shape[0] * 8) ** 0.5)
    return gram_basis(own_rows, scale)


def solution(mesh):
    placed = (
        P("row", "col", None, None, None),
        P("row", "col", None, None),
        P("row", "col"),
        P(("row", "col"), None),
    )
    return jax.shard_map(
        local, mesh=mesh, in_specs=placed, out_specs=P(("col", "row"), None), check_vma=False
    )
```

```python
import jax
import jax.numpy as jnp
from jax import lax
from jax.experimental import pallas as pl
from jax.experimental.pallas import tpu as pltpu
from jax.sharding import PartitionSpec as P

F32 = jnp.float32
BF16 = jnp.bfloat16
HI = lax.Precision.HIGHEST
TILE = 256
NB = 8
K = 512
SLOTS = 48
VMEM = pltpu.VMEM
SMEM = pltpu.SMEM
MESH = pl.DeviceIdType.MESH

CHIPS = 16
DEPTH = 8
NQ = 4
W = 128
BLOCKS = [(i, j) for i in range(4) for j in range(i, 4)]
WHERE = {ij: n * 128 for n, ij in enumerate(BLOCKS)}
HALF = 640
PIECE = 40


def mm(a, b, dims):
    return lax.dot_general(a, b, (dims, ((), ())), precision=HI, preferred_element_type=F32)


def factor(w_ref, b):
    n = 128
    sub = lax.broadcasted_iota(jnp.int32, (b, 128), 0)
    for c0 in range(0, n, b):
        left = w_ref[c0:c0 + b, :128]
        right = w_ref[c0:c0 + b, 128:]
        cols = [jnp.broadcast_to(left[:, c0 + j:c0 + j + 1], (b, 128)) for j in range(b)]
        pivots = jnp.ones((b, 128), F32)
        for j in range(b):
            pivot = cols[j][j:j + 1, :]
            f = jnp.where(sub > j, cols[j] * (1.0 / pivot), 0.0)
            for m in range(j + 1, b):
                cols[m] = cols[m] - f * cols[m][j:j + 1, :]
            if j < b - 1:
                left = left - f * left[j:j + 1, :]
                right = right - f * right[j:j + 1, :]
            pivots = jnp.where(sub == j, pivot, pivots)
        norm = lax.rsqrt(pivots)
        left = left * norm
        right = right * norm
        w_ref[c0:c0 + b, :128] = left
        w_ref[c0:c0 + b, 128:] = right
        e = c0 + b
        if e < n:
            both = jnp.concatenate([left, right], axis=1)
            t = mm(left, both, ((0,), (0,)))
            w_ref[e:, :] = w_ref[e:, :] - t[e:, :]


def gram_kernel(scale, rows_ref, out_ref, mine, twin, parts, planes, gram, x_ref, s_ref, w_ref,
                pair_send, pair_recv, part_send, part_recv, plane_send, plane_recv, gather_send, gather_recv):
    row, z = lax.axis_index("row"), lax.axis_index("col")
    chip, core = row // 2, row % 2
    other = 1 - core

    def at_chip(i):
        return (lax.rem(chip + i, CHIPS) * 2 + core, z)

    def at_plane(i):
        return (row, lax.rem(z + i, DEPTH))

    twin_id = (chip * 2 + other, z)
    barrier = pltpu.get_barrier_semaphore()

    def hello_chip(i, c):
        pl.semaphore_signal(barrier, inc=1, device_id=at_chip(i), device_id_type=MESH)
        return c

    def hello_plane(i, c):
        pl.semaphore_signal(barrier, inc=1, device_id=at_plane(i), device_id_type=MESH)
        return c

    pl.semaphore_signal(barrier, inc=1, device_id=twin_id, device_id_type=MESH)
    lax.fori_loop(1, CHIPS, hello_chip, 0)
    lax.fori_loop(1, DEPTH, hello_plane, 0)

    for i in range(4):
        g = mm(rows_ref[:, i * 128:(i + 1) * 128], rows_ref[:, i * 128:], ((0,), (0,)))
        for j in range(i, 4):
            at = WHERE[i, j]
            mine[at:at + 128, :] = g[:, (j - i) * 128:(j - i + 1) * 128]
    pl.semaphore_wait(barrier, 1 + CHIPS - 1 + DEPTH - 1)

    copy = pltpu.make_async_remote_copy(
        src_ref=mine.at[pl.ds(pl.multiple_of(other * HALF, 8), HALF)], dst_ref=twin,
        send_sem=pair_send.at[0], recv_sem=pair_recv.at[0], device_id=twin_id, device_id_type=MESH)
    copy.start()
    copy.wait()
    own = pl.ds(pl.multiple_of(core * HALF, 8), HALF)
    twin[...] = twin[...] + mine[own, :]

    def part(i):
        there = lax.rem(chip + i, CHIPS)
        return pltpu.make_async_remote_copy(
            src_ref=twin.at[pl.ds(pl.multiple_of(there * PIECE, 8), PIECE)], dst_ref=parts.at[i],
            send_sem=part_send.at[i], recv_sem=part_recv.at[i], device_id=at_chip(i), device_id_type=MESH)

    def start_part(i, c):
        part(i).start()
        return c

    lax.fori_loop(1, CHIPS, start_part, 0)

    def add_part(i, total):
        part(i).wait()
        return total + parts[i]

    total = lax.fori_loop(1, CHIPS, add_part, twin[pl.ds(pl.multiple_of(chip * PIECE, 8), PIECE), :])

    planes[z] = total

    def plane(i):
        return pltpu.make_async_remote_copy(
            src_ref=planes.at[z], dst_ref=planes.at[z],
            send_sem=plane_send.at[i], recv_sem=plane_recv.at[i], device_id=at_plane(i), device_id_type=MESH)

    def start_plane(i, c):
        plane(i).start()
        return c

    def wait_plane(i, c):
        plane(i).wait_send()
        came = lax.rem(z + DEPTH - i, DEPTH)
        pltpu.make_async_remote_copy(
            src_ref=planes.at[came], dst_ref=planes.at[came],
            send_sem=plane_send.at[i], recv_sem=plane_recv.at[i], device_id=at_plane(i), device_id_type=MESH).wait_recv()
        return c

    lax.fori_loop(1, DEPTH, start_plane, 0)
    lax.fori_loop(1, DEPTH, wait_plane, 0)
    total = planes[0]
    for i in range(1, DEPTH):
        total = total + planes[i]

    def slot(n):
        return pl.ds(pl.multiple_of(core * HALF + n * PIECE, 8), PIECE)

    gram[slot(chip), :] = total

    def start_gather(i, c):
        pltpu.make_async_remote_copy(
            src_ref=gram.at[slot(chip)], dst_ref=gram.at[slot(chip)],
            send_sem=gather_send.at[i], recv_sem=gather_recv.at[i], device_id=at_chip(i), device_id_type=MESH).start()
        return c

    def wait_gather(i, c):
        came = lax.rem(chip + CHIPS - i, CHIPS)
        pltpu.make_async_remote_copy(
            src_ref=gram.at[slot(came)], dst_ref=gram.at[slot(came)],
            send_sem=gather_send.at[i], recv_sem=gather_recv.at[i], device_id=at_chip(i), device_id_type=MESH).wait()
        return c

    lax.fori_loop(1, CHIPS, start_gather, 0)
    lax.fori_loop(1, CHIPS, wait_gather, 0)
    there = pl.ds(pl.multiple_of(other * HALF, 8), HALF)
    copy = pltpu.make_async_remote_copy(
        src_ref=gram.at[own], dst_ref=gram.at[own],
        send_sem=pair_send.at[1], recv_sem=pair_recv.at[1], device_id=twin_id, device_id_type=MESH)
    copy.start()
    copy.wait_send()
    pltpu.make_async_remote_copy(
        src_ref=gram.at[there], dst_ref=gram.at[there],
        send_sem=pair_send.at[1], recv_sem=pair_recv.at[1], device_id=twin_id, device_id_type=MESH).wait_recv()

    eye = (
        lax.broadcasted_iota(jnp.int32, (128, 128), 0)
        == lax.broadcasted_iota(jnp.int32, (128, 128), 1)
    ).astype(F32)
    for i, j in BLOCKS:
        at = WHERE[i, j]
        s_ref[i * 128:(i + 1) * 128, j * 128:(j + 1) * 128] = gram[at:at + 128, :]
    x_ref[...] = rows_ref[...]
    for i in range(4):
        lo, hi = i * 128, (i + 1) * 128
        w_ref[:, :128] = s_ref[lo:hi, lo:hi]
        w_ref[:, 128:] = eye
        factor(w_ref, 16)
        inv = w_ref[:, 128:]
        x = mm(x_ref[:, lo:hi], inv, ((1,), (1,)))
        out_ref[:, lo:hi] = x * scale
        if hi < K:
            u = mm(inv, s_ref[lo:hi, hi:], ((1,), (0,)))
            for j in range(i + 1, 4):
                a, b = j * 128, (j + 1) * 128
                s_ref[a:b, a:] = s_ref[a:b, a:] - mm(u[:, a - hi:b - hi], u[:, a - hi:], ((0,), (0,)))
            x_ref[:, hi:] = x_ref[:, hi:] - mm(x, u, ((1,), (0,)))


def gram_basis(rows, scale):
    dma = pltpu.SemaphoreType.DMA
    return pl.pallas_call(
        lambda *refs: gram_kernel(scale, *refs),
        out_shape=jax.ShapeDtypeStruct(rows.shape, F32),
        in_specs=[pl.BlockSpec(memory_space=VMEM)],
        out_specs=pl.BlockSpec(memory_space=VMEM),
        scratch_shapes=[
            VMEM((2 * HALF, 128), F32), VMEM((HALF, 128), F32), VMEM((CHIPS, PIECE, 128), F32),
            VMEM((DEPTH, PIECE, 128), F32), VMEM((2 * HALF, 128), F32), VMEM((64, K), F32),
            VMEM((K, K), F32), VMEM((128, 256), F32),
            dma((2,)), dma((2,)), dma((CHIPS,)), dma((CHIPS,)), dma((DEPTH,)), dma((DEPTH,)), dma((CHIPS,)), dma((CHIPS,)),
        ],
        compiler_params=pltpu.CompilerParams(
            vmem_limit_bytes=40 * 2**20, collective_id=1, has_side_effects=True),
        name="gram_basis",
    )(rows)


def product_kernel(slot_ref, tiles_hbm, panel_ref, out_ref, tiles_ref, at_ref, pan, part, twin, near, far, final, last,
                   tile_sem, ring_send, ring_recv, pair_send, pair_recv, near_send, near_recv,
                   far_send, far_recv, last_send, last_recv):
    row, z = lax.axis_index("row"), lax.axis_index("col")
    core, x, y = row % 2, (row // 2) % 4, row // 8
    other = 1 - core

    def device(yy, xx, cc, zz):
        return ((yy * 4 + xx) * 2 + cc, zz)

    def ring4(v, step):
        return lax.rem(v + step + 4, 4)

    up = device(y, x, core, lax.rem(z + 1, DEPTH))
    down = device(y, x, core, lax.rem(z + DEPTH - 1, DEPTH))
    twin_id = device(y, x, other, z)

    def along(axis, step):
        return device(y, ring4(x, step), core, z) if axis == 0 else device(ring4(y, step), x, core, z)

    barrier = pltpu.get_barrier_semaphore()
    peers = [up, down, twin_id] + [along(a, s) for a in (0, 1) for s in (1, 2, 3)]
    for peer in peers:
        pl.semaphore_signal(barrier, inc=1, device_id=peer, device_id_type=MESH)
    fetch = pltpu.make_async_copy(tiles_hbm, tiles_ref, tile_sem)
    fetch.start()
    for q in range(NQ):
        pan[q, z] = panel_ref[:, q * W:(q + 1) * W]
    pl.semaphore_wait(barrier, len(peers))

    def remote(src, dst, send, recv, peer):
        return pltpu.make_async_remote_copy(
            src_ref=src, dst_ref=dst, send_sem=send, recv_sem=recv, device_id=peer, device_id_type=MESH)

    def hop(q, h, way):
        block = lax.rem(z - h + DEPTH, DEPTH) if way == 0 else lax.rem(z + h, DEPTH)
        ref = pan.at[q, block]
        if h == 3:
            ref = ref.at[pl.ds(0, TILE // 2)] if way == 0 else ref.at[pl.ds(TILE // 2, TILE // 2)]
        return remote(ref, ref, ring_send.at[way, q, h], ring_recv.at[way, q, h], up if way == 0 else down)

    def came(q, h, way):
        block = lax.rem(z - 1 - h + DEPTH, DEPTH) if way == 0 else lax.rem(z + 1 + h, DEPTH)
        ref = pan.at[q, block]
        if h == 3:
            ref = ref.at[pl.ds(0, TILE // 2)] if way == 0 else ref.at[pl.ds(TILE // 2, TILE // 2)]
        remote(ref, ref, ring_send.at[way, q, h], ring_recv.at[way, q, h], up if way == 0 else down).wait_recv()

    def slot(s):
        q, h = 2 * (s // 8) + s % 2, (s % 8) // 2
        for way in (0, 1):
            if h > 0:
                came(q, h - 1, way)
            hop(q, h, way).start()

    def build(b):
        def one(i, carry):
            n = slot_ref[b * NB + i]
            tile = tiles_ref[jnp.minimum(n, SLOTS - 1)]
            tile = jnp.where(n < SLOTS, tile, jnp.zeros_like(tile)).T
            for xl in range(2):
                for c in range(2):
                    at = (xl * 2 + c) * 64
                    to = pl.multiple_of((2 * (i % 2) + xl) * 64, 64)
                    at_ref[b, c, i // 2, pl.ds(to, 64), :] = tile[at:at + 64, :]
            return carry

        lax.fori_loop(0, NB, one, 0)

    def multiply(q, c):
        def one(m, carry):
            total = jnp.dot(at_ref[0, c, m], pan[q, 0], preferred_element_type=F32)
            for b in range(1, NB):
                total += jnp.dot(at_ref[b, c, m], pan[q, b], preferred_element_type=F32)
            for xx in range(4):
                piece = total[xx * 64:(xx + 1) * 64, :]
                if q % 2 == 0:
                    part[q, c, xx, m] = piece
                else:
                    part[q, c, m, xx] = piece
            return carry

        lax.fori_loop(0, 4, one, 0)

    def to_twin(q):
        return remote(part.at[q, other], twin.at[q], pair_send.at[q], pair_recv.at[q], twin_id)

    def compute(q):
        came(q, 3, 0)
        came(q, 3, 1)
        multiply(q, other)
        to_twin(q).start()
        multiply(q, core)

    def here(q):
        return x if q % 2 == 0 else y

    def near_copy(q, n):
        step, half = ((2, 0), (1, 2), (2, 2), (-1, 0))[n]
        ref = twin.at[q, ring4(here(q), step), pl.ds(half, 2)]
        return remote(ref, near.at[q, n], near_send.at[q, n], near_recv.at[q, n], along(q % 2, 1 if n < 2 else -1))

    def far_copy(q, n):
        return remote(near.at[q, 2 * n], far.at[q, n], far_send.at[q, n], far_recv.at[q, n], along(q % 2, 1 - 2 * n))

    def stage1(q):
        to_twin(q).wait_recv()
        twin[q] = twin[q] + part[q, core]
        for n in range(4):
            near_copy(q, n).start()

    def stage2(q):
        u = here(q)
        near_copy(q, 0).wait_recv()
        near[q, 0] = near[q, 0] + twin[q, ring4(u, 1), 0:2]
        far_copy(q, 0).start()
        near_copy(q, 2).wait_recv()
        near[q, 2] = near[q, 2] + twin[q, ring4(u, -1), 2:4]
        far_copy(q, 1).start()

    def last_copy(q, s):
        return remote(final.at[q, ring4(here(q + 1), s)], last.at[q, s], last_send.at[q, s], last_recv.at[q, s], along(1 - q % 2, s))

    def stage3(q):
        u = here(q)
        near_copy(q, 1).wait_recv()
        near_copy(q, 3).wait_recv()
        far_copy(q, 0).wait_recv()
        final[q, 0:2] = twin[q, u, 0:2] + near[q, 3] + far[q, 0]
        far_copy(q, 1).wait_recv()
        final[q, 2:4] = twin[q, u, 2:4] + near[q, 1] + far[q, 1]
        for s in (1, 2, 3):
            last_copy(q, s).start()

    def stage4(q):
        v = here(q + 1)
        for s in (1, 2, 3):
            last_copy(q, s).wait_recv()
        out_ref[:, q * W:(q + 1) * W] = final[q, v] + last[q, 1] + last[q, 2] + last[q, 3]

    slot(0)
    slot(1)
    fetch.wait()
    build(0)
    for s in range(2, 8):
        slot(s)
        build(s - 1)
    build(7)
    slot(8)
    slot(9)
    compute(0)
    slot(10)
    compute(1)
    slot(11)
    stage1(0)
    slot(12)
    stage1(1)
    slot(13)
    stage2(0)
    slot(14)
    stage2(1)
    slot(15)
    stage3(0)
    stage3(1)
    compute(2)
    compute(3)
    stage4(0)
    stage4(1)
    for stage in (stage1, stage2, stage3, stage4):
        stage(2)
        stage(3)

    for q in range(NQ):
        for h in range(4):
            for way in (0, 1):
                hop(q, h, way).wait_send()
        to_twin(q).wait_send()
        for n in range(4):
            near_copy(q, n).wait_send()
        for n in range(2):
            far_copy(q, n).wait_send()
        for s in (1, 2, 3):
            last_copy(q, s).wait_send()


def product_rows(slot_of, tiles, panel):
    dma = pltpu.SemaphoreType.DMA
    return pl.pallas_call(
        product_kernel,
        out_shape=jax.ShapeDtypeStruct((64, K), F32),
        in_specs=[
            pl.BlockSpec(memory_space=SMEM),
            pl.BlockSpec(memory_space=pl.ANY),
            pl.BlockSpec(memory_space=VMEM),
        ],
        out_specs=pl.BlockSpec(memory_space=VMEM),
        scratch_shapes=[
            VMEM((SLOTS, TILE, TILE), BF16),
            VMEM((NB, 2, 4, TILE, TILE), BF16),
            VMEM((NQ, DEPTH, TILE, W), BF16),
            VMEM((NQ, 2, 4, 4, 64, W), F32),
            VMEM((NQ, 4, 4, 64, W), F32),
            VMEM((NQ, 4, 2, 64, W), F32),
            VMEM((NQ, 2, 2, 64, W), F32),
            VMEM((NQ, 4, 64, W), F32),
            VMEM((NQ, 4, 64, W), F32),
            dma, dma((2, NQ, 4)), dma((2, NQ, 4)), dma((NQ,)), dma((NQ,)), dma((NQ, 4)), dma((NQ, 4)),
            dma((NQ, 2)), dma((NQ, 2)), dma((NQ, 4)), dma((NQ, 4)),
        ],
        compiler_params=pltpu.CompilerParams(
            vmem_limit_bytes=56 * 2**20, collective_id=0, has_side_effects=True),
        name="product_rows",
    )(slot_of, tiles, panel)


def local(tiles, coords, counts, panel):
    where = coords[0, 0]
    position = where[:, 0] * NB + where[:, 1]
    slots = jnp.arange(SLOTS, dtype=jnp.int32)
    live = slots < counts[0, 0]
    match = (position[None, :] == jnp.arange(NB * NB, dtype=jnp.int32)[:, None]) & live[None, :]
    slot_of = jnp.min(jnp.where(match, slots[None, :], SLOTS), axis=1)

    own_rows = product_rows(slot_of, tiles[0, 0], panel)
    scale = float((NB * TILE * DEPTH) ** 0.5)
    return gram_basis(own_rows, scale)


def solution(mesh):
    placed = (
        P("row", "col", None, None, None),
        P("row", "col", None, None),
        P("row", "col"),
        P(("row", "col"), None),
    )
    return jax.shard_map(
        local, mesh=mesh, in_specs=placed, out_specs=P(("col", "row"), None), check_vma=False
    )
```

```python
import jax
import jax.numpy as jnp
from jax import lax
from jax.experimental import pallas as pl
from jax.experimental.pallas import tpu as pltpu
from jax.sharding import PartitionSpec as P

F32 = jnp.float32
BF16 = jnp.bfloat16
HI = lax.Precision.HIGHEST
MESH = pl.DeviceIdType.MESH
VMEM = pltpu.VMEM
SMEM = pltpu.SMEM
TILE = 256
NB = 8
K = 512
SLOTS = 48
CHIPS = 16
DEPTH = 8
W = 128
NQ = 4
OWN = 64
PANEL = 16


def mm(a, b, dims):
    return lax.dot_general(a, b, (dims, ((), ())), precision=HI, preferred_element_type=F32)


def split(v):
    hi = v.astype(BF16)
    rest = v - hi.astype(F32)
    mid = rest.astype(BF16)
    return hi, mid, (rest - mid.astype(F32)).astype(BF16)


def stacked(a, b):
    ah, am, al = split(a)
    bh, bm, bl = split(b)
    return lax.dot_general(
        jnp.concatenate([ah, ah, am, am, ah, al], axis=0),
        jnp.concatenate([bh, bm, bh, bm, bl, bh], axis=0),
        (((0,), (0,)), ((), ())),
        preferred_element_type=F32,
    )


def factor(w):
    sub = lax.broadcasted_iota(jnp.int32, (PANEL, W), 0)
    rows = [w[c:c + PANEL, :] for c in range(0, W, PANEL)]
    for k in range(W // PANEL):
        c0 = k * PANEL
        left, right = rows[k][:, :W], rows[k][:, W:]
        cols = [jnp.broadcast_to(left[:, c0 + j:c0 + j + 1], (PANEL, W)) for j in range(PANEL)]
        pivots = jnp.ones((PANEL, W), F32)
        for j in range(PANEL):
            pivot = cols[j][j:j + 1, :]
            f = jnp.where(sub > j, cols[j] * (1.0 / pivot), 0.0)
            for m in range(j + 1, PANEL):
                cols[m] = cols[m] - f * cols[m][j:j + 1, :]
            if j < PANEL - 1:
                left = left - f * left[j:j + 1, :]
                right = right - f * right[j:j + 1, :]
            pivots = jnp.where(sub == j, pivot, pivots)
        norm = lax.rsqrt(pivots)
        left = left * norm
        rows[k] = jnp.concatenate([left, right * norm], axis=1)
        if c0 + PANEL < W:
            t = stacked(left, rows[k])
            for m in range(k + 1, W // PANEL):
                rows[m] = rows[m] - t[m * PANEL:(m + 1) * PANEL, :]
        yield
    return jnp.concatenate(rows, axis=0)


def fused_kernel(scale, slot_ref, tiles_hbm, panel_ref, out_ref, tiles_ref, at_ref, pan, part, twin, near, far, final,
                 last, x_ref, s_ref, u_ref, *rest):
    bufs = (rest[0:5], rest[5:10])
    (tile_sem, ring_send, ring_recv, pair_send, pair_recv, near_send, near_recv, far_send, far_recv,
     last_send, last_recv) = rest[10:21]
    sems = (rest[21:29], rest[29:37])
    row, z = lax.axis_index("row"), lax.axis_index("col")
    core, chip = row % 2, row // 2
    x, y = chip % 4, chip // 4
    other = 1 - core

    def device(yy, xx, cc, zz):
        return ((yy * 4 + xx) * 2 + cc, zz)

    def ring4(v, step):
        return lax.rem(v + step + 4, 4)

    def at_chip(i):
        return (lax.rem(chip + i, CHIPS) * 2 + core, z)

    def at_plane(i):
        return (row, lax.rem(z + i, DEPTH))

    up, down = at_plane(1), at_plane(DEPTH - 1)
    twin_id = device(y, x, other, z)

    def along(axis, step):
        return device(y, ring4(x, step), core, z) if axis == 0 else device(ring4(y, step), x, core, z)

    def hello(device_of):
        def one(i, carry):
            pl.semaphore_signal(barrier, inc=1, device_id=device_of(i), device_id_type=MESH)
            return carry
        return one

    barrier = pltpu.get_barrier_semaphore()
    lax.fori_loop(1, DEPTH, hello(at_plane), 0)
    lax.fori_loop(1, CHIPS, hello(at_chip), 0)
    pl.semaphore_signal(barrier, inc=1, device_id=twin_id, device_id_type=MESH)
    fetch = pltpu.make_async_copy(tiles_hbm, tiles_ref, tile_sem)
    fetch.start()
    for p in range(2):
        pan[p, z] = panel_ref[:, p * TILE:(p + 1) * TILE]
    pl.semaphore_wait(barrier, DEPTH - 1 + CHIPS - 1 + 1)

    def remote(src, dst, send, recv, peer):
        return pltpu.make_async_remote_copy(
            src_ref=src, dst_ref=dst, send_sem=send, recv_sem=recv, device_id=peer, device_id_type=MESH)

    def ring_copy(p, a, h, way, block):
        ref = pan.at[p, block, pl.ds(a * 64, 64)]
        return remote(ref, ref, ring_send.at[way, p, a, h], ring_recv.at[way, p, a, h], up if way == 0 else down)

    def hop(p, a, h, way):
        return ring_copy(p, a, h, way, lax.rem(z + (DEPTH - h if way == 0 else h), DEPTH))

    def came(p, a, h, way):
        ring_copy(p, a, h, way, lax.rem(z + (DEPTH - 1 - h if way == 0 else 1 + h), DEPTH)).wait_recv()

    def ring(p, a, h):
        for way in (0, 1):
            piece = a + 2 if h == 3 and way == 1 else a
            if h > 0:
                came(p, piece, h - 1, way)
            hop(p, piece, h, way).start()

    def finish(p):
        for a in (0, 1):
            came(p, a + 2, 2, 0)
            came(p, a, 2, 1)
            came(p, a, 3, 0)
            came(p, a + 2, 3, 1)

    def build(part_of):
        b, first = part_of // 2, part_of % 2 * 4

        def one(i, carry):
            n = slot_ref[b * NB + i]
            tile = tiles_ref[jnp.minimum(n, SLOTS - 1)]
            tile = jnp.where(n < SLOTS, tile, jnp.zeros_like(tile)).T
            for xl in range(2):
                for c in range(2):
                    at = (xl * 2 + c) * 64
                    to = pl.multiple_of((2 * (i % 2) + xl) * 64, 64)
                    at_ref[b, c, i // 2, pl.ds(to, 64), :] = tile[at:at + 64, :]
            return carry

        lax.fori_loop(first, first + 4, one, 0)

    def pair_copy(q, m):
        if q % 2 == 0:
            src, dst = part.at[q, other, :, m], twin.at[q, :, m]
        else:
            src, dst = part.at[q, other, m], twin.at[q, m]
        return remote(src, dst, pair_send.at[q, m], pair_recv.at[q, m], twin_id)

    def multiply(p, c, m):
        total = jnp.dot(at_ref[0, c, m], pan[p, 0], preferred_element_type=F32)
        for b in range(1, NB):
            total += jnp.dot(at_ref[b, c, m], pan[p, b], preferred_element_type=F32)
        for xx in range(4):
            piece = total[xx * 64:(xx + 1) * 64, :]
            part[2 * p, c, xx, m] = piece[:, :W]
            part[2 * p + 1, c, m, xx] = piece[:, W:]

    def compute_other(p):
        def one(m, carry):
            multiply(p, other, m)
            pair_copy(2 * p, m).start()
            pair_copy(2 * p + 1, m).start()
            return carry
        lax.fori_loop(0, 4, one, 0)

    def compute_own(p):
        def one(m, carry):
            multiply(p, core, m)
            return carry
        lax.fori_loop(0, 4, one, 0)

    def here(q):
        return x if q % 2 == 0 else y

    def near_copy(q, n):
        step, half = ((2, 0), (1, 2), (2, 2), (-1, 0))[n]
        ref = twin.at[q, ring4(here(q), step), pl.ds(half, 2)]
        return remote(ref, near.at[q, n], near_send.at[q, n], near_recv.at[q, n], along(q % 2, 1 if n < 2 else -1))

    def far_copy(q, n):
        return remote(near.at[q, 2 * n], far.at[q, n], far_send.at[q, n], far_recv.at[q, n], along(q % 2, 1 - 2 * n))

    def last_copy(q, s):
        return remote(final.at[q, ring4(here(q + 1), s)], last.at[q, s], last_send.at[q, s], last_recv.at[q, s],
                      along(1 - q % 2, s))

    def stage1(q):
        for m in range(4):
            pair_copy(q, m).wait_recv()
        twin[q] = twin[q] + part[q, core]
        for n in (0, 2, 1, 3):
            near_copy(q, n).start()

    def stage2(q):
        u = here(q)
        near_copy(q, 0).wait_recv()
        near[q, 0] = near[q, 0] + twin[q, ring4(u, 1), 0:2]
        far_copy(q, 0).start()
        near_copy(q, 2).wait_recv()
        near[q, 2] = near[q, 2] + twin[q, ring4(u, -1), 2:4]
        far_copy(q, 1).start()

    def stage3(q):
        u = here(q)
        near_copy(q, 1).wait_recv()
        near_copy(q, 3).wait_recv()
        far_copy(q, 0).wait_recv()
        final[q, 0:2] = twin[q, u, 0:2] + near[q, 3] + far[q, 0]
        far_copy(q, 1).wait_recv()
        final[q, 2:4] = twin[q, u, 2:4] + near[q, 1] + far[q, 1]
        for s in (1, 2, 3):
            last_copy(q, s).start()

    def stage4(q):
        v = here(q + 1)
        for s in (1, 2, 3):
            last_copy(q, s).wait_recv()
        x_ref[:, q * W:(q + 1) * W] = final[q, v] + last[q, 1] + last[q, 2] + last[q, 3]

    def gram_steps(p):
        mine, half, parts, planes, gram = bufs[p]
        two_send, two_recv, part_send, part_recv, plane_send, plane_recv, back_send, back_recv = sems[p]
        deep = TILE * (p + 1)
        size = deep // CHIPS
        own = pl.ds(pl.multiple_of(core * deep, 8), deep)
        away = pl.ds(pl.multiple_of(other * deep, 8), deep)

        def pair(n):
            src, dst = (mine.at[away], half) if n == 0 else (gram.at[own], gram.at[own])
            return remote(src, dst, two_send.at[n], two_recv.at[n], twin_id)

        def chip_copy(i):
            there = lax.rem(chip + i, CHIPS)
            return remote(half.at[pl.ds(pl.multiple_of(there * size, 8), size)], parts.at[i],
                          part_send.at[i], part_recv.at[i], at_chip(i))

        def plane_copy(i, which):
            ref = planes.at[which]
            return remote(ref, ref, plane_send.at[i], plane_recv.at[i], at_plane(i))

        def piece(n):
            return pl.ds(pl.multiple_of(core * deep + n * size, 8), size)

        def back_copy(i, which):
            ref = gram.at[piece(which)]
            return remote(ref, ref, back_send.at[i], back_recv.at[i], at_chip(i))

        def loop(low, high, act):
            def one(i, carry):
                act(i)
                return carry
            lax.fori_loop(low, high, one, 0)

        def local():
            g = mm(x_ref[:, :deep], x_ref[:, p * TILE:(p + 1) * TILE], ((0,), (0,)))
            mine[0:deep, :] = g[:, :W]
            mine[deep:, :] = g[:, W:]
            pair(0).start()

        def to_chips():
            pair(0).wait_recv()
            half[...] = half[...] + mine[own, :]
            loop(1, CHIPS, lambda i: chip_copy(i).start())

        def to_planes():
            def add(i, total):
                chip_copy(i).wait_recv()
                return total + parts[i]
            planes[z] = lax.fori_loop(1, CHIPS, add, half[pl.ds(pl.multiple_of(chip * size, 8), size), :])
            loop(1, DEPTH, lambda i: plane_copy(i, z).start())

        def back():
            loop(1, DEPTH, lambda i: plane_copy(i, lax.rem(z + DEPTH - i, DEPTH)).wait_recv())
            total = planes[0]
            for i in range(1, DEPTH):
                total = total + planes[i]
            gram[piece(chip), :] = total
            loop(1, CHIPS, lambda i: back_copy(i, chip).start())

        def to_pair():
            loop(1, CHIPS, lambda i: back_copy(i, lax.rem(chip + CHIPS - i, CHIPS)).wait_recv())
            pair(1).start()

        def done():
            ref = gram.at[away]
            remote(ref, ref, two_send.at[1], two_recv.at[1], twin_id).wait_recv()
            s_ref[0:deep, p * TILE:p * TILE + W] = gram[0:deep, :]
            s_ref[0:deep, p * TILE + W:(p + 1) * TILE] = gram[deep:, :]

        def sent():
            pair(0).wait_send()
            pair(1).wait_send()
            loop(1, CHIPS, lambda i: chip_copy(i).wait_send())
            loop(1, DEPTH, lambda i: plane_copy(i, z).wait_send())
            loop(1, CHIPS, lambda i: back_copy(i, chip).wait_send())

        return local, to_chips, to_planes, back, to_pair, done, sent

    eye = (lax.broadcasted_iota(jnp.int32, (W, W), 0) == lax.broadcasted_iota(jnp.int32, (W, W), 1)).astype(F32)

    def solve(p):
        a, b, e = p * TILE, p * TILE + W, (p + 1) * TILE
        w = yield from factor(jnp.concatenate([s_ref[a:b, a:b], eye], axis=1))
        inv = w[:, W:]
        first = mm(x_ref[:, a:b], inv, ((1,), (1,)))
        out_ref[:, a:b] = first * scale
        u = mm(inv, s_ref[a:b, b:e], ((1,), (0,)))
        s_ref[b:e, b:e] = s_ref[b:e, b:e] - mm(u, u, ((0,), (0,)))
        w = yield from factor(jnp.concatenate([s_ref[b:e, b:e], eye], axis=1))
        inv2 = w[:, W:]
        second = mm(x_ref[:, b:e] - mm(first, u, ((1,), (0,))), inv2, ((1,), (1,)))
        out_ref[:, b:e] = second * scale
        if p == 0:
            x_ref[:, a:b] = first
            x_ref[:, b:e] = second
            u_ref[0:W, 0:W] = inv
            u_ref[0:W, W:] = jnp.zeros_like(inv)
            u_ref[W:, 0:W] = -mm(inv2, mm(u, inv, ((0,), (0,))), ((1,), (0,)))
            u_ref[W:, W:] = inv2

    def couple():
        u = mm(u_ref[...], s_ref[:TILE, TILE:], ((1,), (0,)))
        s_ref[TILE:, TILE:] = s_ref[TILE:, TILE:] - mm(u, u, ((0,), (0,)))
        x_ref[:, TILE:] = x_ref[:, TILE:] - mm(x_ref[:, :TILE], u, ((1,), (0,)))

    def run(*acts):
        for act in acts:
            act[0](*act[1:])

    for a in range(4):
        ring(0, a, 0)
    ring(1, 0, 0)
    fetch.wait()
    run((build, 0), (build, 1), (build, 2), (build, 3))
    for a in range(4):
        run((ring, 0, a, 1), (build, 4 + a))
    ring(1, 1, 0)
    build(8)
    for a in range(4):
        run((ring, 0, a, 2), (build, 9 + a))
    run((ring, 1, 2, 0), (ring, 1, 0, 1), (build, 13))
    run((ring, 0, 0, 3), (build, 14), (ring, 0, 1, 3), (build, 15))
    run((ring, 1, 3, 0), (ring, 1, 1, 1), (finish, 0), (ring, 1, 2, 1))
    compute_other(0)
    run((ring, 1, 3, 1), (ring, 1, 0, 2))
    compute_own(0)
    run((ring, 1, 1, 2), (stage1, 0), (stage1, 1), (ring, 1, 2, 2), (ring, 1, 3, 2))
    run((stage2, 0), (stage2, 1), (ring, 1, 0, 3), (ring, 1, 1, 3), (stage3, 0), (stage3, 1))
    finish(1)
    compute_other(1)
    run((stage4, 0), (stage4, 1))
    early, late = gram_steps(0), gram_steps(1)
    early[0]()
    compute_own(1)
    run((stage1, 2), (stage1, 3))
    early[1]()
    run((stage2, 2), (stage2, 3))
    early[2]()
    run((stage3, 2), (stage3, 3))
    early[3]()
    run((stage4, 2), (stage4, 3))
    late[0]()
    early[4]()
    late[1]()
    early[5]()
    for n, _ in enumerate(solve(0)):
        if n in (4, 8, 12):
            late[2 + n // 4 - 1]()
    late[5]()
    couple()
    for _ in solve(1):
        pass

    for p in range(2):
        for h in range(4):
            for a in range(2 if h == 3 else 4):
                for way in (0, 1):
                    hop(p, a + 2 if h == 3 and way == 1 else a, h, way).wait_send()
    for q in range(NQ):
        for n in range(4):
            pair_copy(q, n).wait_send()
            near_copy(q, n).wait_send()
        for n in range(2):
            far_copy(q, n).wait_send()
        for s in (1, 2, 3):
            last_copy(q, s).wait_send()
    early[6]()
    late[6]()


def basis_of(slot_of, tiles, panel, scale):
    dma = pltpu.SemaphoreType.DMA

    def gram_buffers(p):
        deep = TILE * (p + 1)
        size = deep // CHIPS
        return [VMEM((2 * deep, W), F32), VMEM((deep, W), F32), VMEM((CHIPS, size, W), F32),
                VMEM((DEPTH, size, W), F32), VMEM((2 * deep, W), F32)]

    gram_sems = [dma((2,)), dma((2,)), dma((CHIPS,)), dma((CHIPS,)), dma((DEPTH,)), dma((DEPTH,)),
                 dma((CHIPS,)), dma((CHIPS,))]
    return pl.pallas_call(
        lambda *refs: fused_kernel(scale, *refs),
        out_shape=jax.ShapeDtypeStruct((OWN, K), F32),
        in_specs=[
            pl.BlockSpec(memory_space=SMEM),
            pl.BlockSpec(memory_space=pl.ANY),
            pl.BlockSpec(memory_space=VMEM),
        ],
        out_specs=pl.BlockSpec(memory_space=VMEM),
        scratch_shapes=[
            VMEM((SLOTS, TILE, TILE), BF16),
            VMEM((NB, 2, 4, TILE, TILE), BF16),
            VMEM((2, DEPTH, TILE, TILE), BF16),
            VMEM((NQ, 2, 4, 4, OWN, W), F32),
            VMEM((NQ, 4, 4, OWN, W), F32),
            VMEM((NQ, 4, 2, OWN, W), F32),
            VMEM((NQ, 2, 2, OWN, W), F32),
            VMEM((NQ, 4, OWN, W), F32),
            VMEM((NQ, 4, OWN, W), F32),
            VMEM((OWN, K), F32),
            VMEM((K, K), F32),
            VMEM((TILE, TILE), F32),
            *gram_buffers(0),
            *gram_buffers(1),
            dma, dma((2, 2, 4, 4)), dma((2, 2, 4, 4)), dma((NQ, 4)), dma((NQ, 4)), dma((NQ, 4)), dma((NQ, 4)),
            dma((NQ, 2)), dma((NQ, 2)), dma((NQ, 4)), dma((NQ, 4)),
            *gram_sems,
            *gram_sems,
        ],
        compiler_params=pltpu.CompilerParams(
            vmem_limit_bytes=56 * 2**20, collective_id=0, has_side_effects=True),
        name="panel_basis",
    )(slot_of, tiles, panel)


def local(tiles, coords, counts, panel):
    where = coords[0, 0]
    position = where[:, 0] * NB + where[:, 1]
    slots = jnp.arange(SLOTS, dtype=jnp.int32)
    live = slots < counts[0, 0]
    match = (position[None, :] == jnp.arange(NB * NB, dtype=jnp.int32)[:, None]) & live[None, :]
    slot_of = jnp.min(jnp.where(match, slots[None, :], SLOTS), axis=1)
    scale = float((NB * TILE * DEPTH) ** 0.5)
    return basis_of(slot_of, tiles[0, 0], panel, scale)


def solution(mesh):
    placed = (
        P("row", "col", None, None, None),
        P("row", "col", None, None),
        P("row", "col"),
        P(("row", "col"), None),
    )
    return jax.shard_map(
        local, mesh=mesh, in_specs=placed, out_specs=P(("col", "row"), None), check_vma=False
    )
```

```python
import jax
import jax.numpy as jnp
from jax import lax
from jax.experimental import pallas as pl
from jax.experimental.pallas import tpu as pltpu
from jax.sharding import PartitionSpec as P

F32 = jnp.float32
BF16 = jnp.bfloat16
HI = lax.Precision.HIGHEST
MESH = pl.DeviceIdType.MESH
VMEM = pltpu.VMEM
SMEM = pltpu.SMEM
TILE = 256
NB = 8
K = 512
SLOTS = 48
CHIPS = 16
DEPTH = 8
W = 128
NQ = 4
OWN = 64
PANEL = 16


def mm(a, b, dims):
    return lax.dot_general(a, b, (dims, ((), ())), precision=HI, preferred_element_type=F32)


def split(v):
    hi = v.astype(BF16)
    rest = v - hi.astype(F32)
    mid = rest.astype(BF16)
    return hi, mid, (rest - mid.astype(F32)).astype(BF16)


def stacked(a, b):
    ah, am, al = split(a)
    bh, bm, bl = split(b)
    return lax.dot_general(
        jnp.concatenate([ah, ah, am, am, ah, al], axis=0),
        jnp.concatenate([bh, bm, bh, bm, bl, bh], axis=0),
        (((0,), (0,)), ((), ())),
        preferred_element_type=F32,
    )


def factor(w):
    sub = lax.broadcasted_iota(jnp.int32, (PANEL, W), 0)
    rows = [w[c:c + PANEL, :] for c in range(0, W, PANEL)]
    for k in range(W // PANEL):
        c0 = k * PANEL
        left, right = rows[k][:, :W], rows[k][:, W:]
        cols = [jnp.broadcast_to(left[:, c0 + j:c0 + j + 1], (PANEL, W)) for j in range(PANEL)]
        pivots = jnp.ones((PANEL, W), F32)
        for j in range(PANEL):
            pivot = cols[j][j:j + 1, :]
            f = jnp.where(sub > j, cols[j] * (1.0 / pivot), 0.0)
            for m in range(j + 1, PANEL):
                cols[m] = cols[m] - f * cols[m][j:j + 1, :]
            if j < PANEL - 1:
                left = left - f * left[j:j + 1, :]
                right = right - f * right[j:j + 1, :]
            pivots = jnp.where(sub == j, pivot, pivots)
        norm = lax.rsqrt(pivots)
        left = left * norm
        rows[k] = jnp.concatenate([left, right * norm], axis=1)
        if c0 + PANEL < W:
            t = stacked(left, rows[k])
            for m in range(k + 1, W // PANEL):
                rows[m] = rows[m] - t[m * PANEL:(m + 1) * PANEL, :]
        yield
    return jnp.concatenate(rows, axis=0)


def fused_kernel(scale, coords_ref, count_ref, tiles_hbm, panel_hbm, out_ref, slot_vec, slot_ref, tiles_ref, at_ref, pan, part, twin, near, far, final,
                 last, x_ref, s_ref, u_ref, *rest):
    bufs = (rest[0:5], rest[5:10])
    (slot_sem, panel_sem, tile_sem, ring_send, ring_recv, pair_send, pair_recv, near_send, near_recv, far_send, far_recv,
     last_send, last_recv) = rest[10:23]
    sems = (rest[23:31], rest[31:39])
    row, z = lax.axis_index("row"), lax.axis_index("col")
    core, chip = row % 2, row // 2
    x, y = chip % 4, chip // 4
    other = 1 - core

    def device(yy, xx, cc, zz):
        return ((yy * 4 + xx) * 2 + cc, zz)

    def ring4(v, step):
        return lax.rem(v + step + 4, 4)

    def at_chip(i):
        return (lax.rem(chip + i, CHIPS) * 2 + core, z)

    def at_plane(i):
        return (row, lax.rem(z + i, DEPTH))

    up, down = at_plane(1), at_plane(DEPTH - 1)
    twin_id = device(y, x, other, z)

    def along(axis, step):
        return device(y, ring4(x, step), core, z) if axis == 0 else device(ring4(y, step), x, core, z)

    def hello(device_of):
        def one(i, carry):
            pl.semaphore_signal(barrier, inc=1, device_id=device_of(i), device_id_type=MESH)
            return carry
        return one

    def block_rows(block, start, count):
        return pl.ds(pl.multiple_of(block * TILE + start, 64), count)

    barrier = pltpu.get_barrier_semaphore()
    lax.fori_loop(1, DEPTH, hello(at_plane), 0)
    lax.fori_loop(1, CHIPS, hello(at_chip), 0)
    pl.semaphore_signal(barrier, inc=1, device_id=twin_id, device_id_type=MESH)
    fetch = pltpu.make_async_copy(tiles_hbm, tiles_ref, tile_sem)
    fetch.start()
    own_panel = [pltpu.make_async_copy(panel_hbm.at[:, pl.ds(p * TILE, TILE)], pan.at[p, block_rows(z, 0, TILE)],
                                       panel_sem.at[p]) for p in range(2)]
    for copy in own_panel:
        copy.start()

    position = coords_ref[0:1, :] * NB + coords_ref[1:2, :]
    slot = lax.broadcasted_iota(jnp.int32, (NB * NB, SLOTS), 1)
    match = (position == lax.broadcasted_iota(jnp.int32, (NB * NB, SLOTS), 0)) & (slot < count_ref[0, 0])
    first = jnp.min(jnp.where(match, slot, SLOTS), axis=1, keepdims=True)
    slot_vec[...] = jnp.broadcast_to(first, (NB * NB, W))
    to_scalars = pltpu.make_async_copy(slot_vec, slot_ref, slot_sem)
    to_scalars.start()
    for copy in own_panel:
        copy.wait()
    pl.semaphore_wait(barrier, DEPTH - 1 + CHIPS - 1 + 1)

    def remote(src, dst, send, recv, peer):
        return pltpu.make_async_remote_copy(
            src_ref=src, dst_ref=dst, send_sem=send, recv_sem=recv, device_id=peer, device_id_type=MESH)

    def ring_copy(p, a, h, way, block):
        ref = pan.at[p, block_rows(block, a * 64, 64)]
        return remote(ref, ref, ring_send.at[way, p, a, h], ring_recv.at[way, p, a, h], up if way == 0 else down)

    def hop(p, a, h, way):
        return ring_copy(p, a, h, way, lax.rem(z + (DEPTH - h if way == 0 else h), DEPTH))

    def came(p, a, h, way):
        ring_copy(p, a, h, way, lax.rem(z + (DEPTH - 1 - h if way == 0 else 1 + h), DEPTH)).wait_recv()

    def ring(p, a, h):
        for way in (0, 1):
            piece = a + 2 if h == 3 and way == 1 else a
            if h > 0:
                came(p, piece, h - 1, way)
            hop(p, piece, h, way).start()

    def finish(p):
        for a in (0, 1):
            came(p, a + 2, 2, 0)
            came(p, a, 2, 1)
            came(p, a, 3, 0)
            came(p, a + 2, 3, 1)

    def build(part_of):
        b, first = part_of // 2, part_of % 2 * 4

        def one(i, carry):
            n = slot_ref[b * NB + i, 0]
            tile = tiles_ref[jnp.minimum(n, SLOTS - 1)]
            tile = jnp.where(n < SLOTS, tile, jnp.zeros_like(tile)).T
            for xl in range(2):
                for c in range(2):
                    at = (xl * 2 + c) * 64
                    to = pl.multiple_of((2 * (i % 2) + xl) * 64, 64)
                    at_ref[c, i // 2, pl.ds(to, 64), b * TILE:(b + 1) * TILE] = tile[at:at + 64, :]
            return carry

        lax.fori_loop(first, first + 4, one, 0)

    def pair_copy(q, m):
        if q % 2 == 0:
            src, dst = part.at[q, other, :, m], twin.at[q, :, m]
        else:
            src, dst = part.at[q, other, m], twin.at[q, m]
        return remote(src, dst, pair_send.at[q, m], pair_recv.at[q, m], twin_id)

    def multiply(p, c, m):
        total = jnp.dot(at_ref[c, m], pan[p], preferred_element_type=F32)
        for xx in range(4):
            piece = total[xx * 64:(xx + 1) * 64, :]
            part[2 * p, c, xx, m] = piece[:, :W]
            part[2 * p + 1, c, m, xx] = piece[:, W:]

    def other_rows(p, m):
        multiply(p, other, m)
        pair_copy(2 * p, m).start()
        pair_copy(2 * p + 1, m).start()

    def own_rows(p, m):
        multiply(p, core, m)

    def here(q):
        return x if q % 2 == 0 else y

    def near_copy(q, n):
        step, half = ((2, 0), (1, 2), (2, 2), (-1, 0))[n]
        ref = twin.at[q, ring4(here(q), step), pl.ds(half, 2)]
        return remote(ref, near.at[q, n], near_send.at[q, n], near_recv.at[q, n], along(q % 2, 1 if n < 2 else -1))

    def far_copy(q, n):
        return remote(near.at[q, 2 * n], far.at[q, n], far_send.at[q, n], far_recv.at[q, n], along(q % 2, 1 - 2 * n))

    def last_copy(q, s):
        return remote(final.at[q, ring4(here(q + 1), s)], last.at[q, s], last_send.at[q, s], last_recv.at[q, s],
                      along(1 - q % 2, s))

    def stage1(q):
        for m in range(4):
            pair_copy(q, m).wait_recv()
        twin[q] = twin[q] + part[q, core]
        for n in (0, 2, 1, 3):
            near_copy(q, n).start()

    def stage2(q):
        u = here(q)
        near_copy(q, 0).wait_recv()
        near[q, 0] = near[q, 0] + twin[q, ring4(u, 1), 0:2]
        far_copy(q, 0).start()
        near_copy(q, 2).wait_recv()
        near[q, 2] = near[q, 2] + twin[q, ring4(u, -1), 2:4]
        far_copy(q, 1).start()

    def stage3(q):
        u = here(q)
        near_copy(q, 1).wait_recv()
        near_copy(q, 3).wait_recv()
        far_copy(q, 0).wait_recv()
        final[q, 0:2] = twin[q, u, 0:2] + near[q, 3] + far[q, 0]
        far_copy(q, 1).wait_recv()
        final[q, 2:4] = twin[q, u, 2:4] + near[q, 1] + far[q, 1]
        for s in (1, 2, 3):
            last_copy(q, s).start()

    def stage4(q):
        v = here(q + 1)
        for s in (1, 2, 3):
            last_copy(q, s).wait_recv()
        x_ref[:, q * W:(q + 1) * W] = final[q, v] + last[q, 1] + last[q, 2] + last[q, 3]

    def gram_steps(p):
        mine, half, parts, planes, gram = bufs[p]
        two_send, two_recv, part_send, part_recv, plane_send, plane_recv, back_send, back_recv = sems[p]
        deep = TILE * (p + 1)
        size = deep // CHIPS
        own = pl.ds(pl.multiple_of(core * deep, 8), deep)
        away = pl.ds(pl.multiple_of(other * deep, 8), deep)

        def pair(n):
            src, dst = (mine.at[away], half) if n == 0 else (gram.at[own], gram.at[own])
            return remote(src, dst, two_send.at[n], two_recv.at[n], twin_id)

        def chip_copy(i):
            there = lax.rem(chip + i, CHIPS)
            return remote(half.at[pl.ds(pl.multiple_of(there * size, 8), size)], parts.at[i],
                          part_send.at[i], part_recv.at[i], at_chip(i))

        def plane_copy(i, which):
            ref = planes.at[which]
            return remote(ref, ref, plane_send.at[i], plane_recv.at[i], at_plane(i))

        def piece(n):
            return pl.ds(pl.multiple_of(core * deep + n * size, 8), size)

        def back_copy(i, which):
            ref = gram.at[piece(which)]
            return remote(ref, ref, back_send.at[i], back_recv.at[i], at_chip(i))

        def loop(low, high, act):
            def one(i, carry):
                act(i)
                return carry
            lax.fori_loop(low, high, one, 0)

        def local():
            g = stacked(x_ref[:, :deep], x_ref[:, p * TILE:(p + 1) * TILE])
            mine[0:deep, :] = g[:, :W]
            mine[deep:, :] = g[:, W:]
            pair(0).start()

        def to_chips():
            pair(0).wait_recv()
            half[...] = half[...] + mine[own, :]
            loop(1, CHIPS, lambda i: chip_copy(i).start())

        def to_planes():
            def add(i, total):
                chip_copy(i).wait_recv()
                return total + parts[i]
            planes[z] = lax.fori_loop(1, CHIPS, add, half[pl.ds(pl.multiple_of(chip * size, 8), size), :])
            loop(1, DEPTH, lambda i: plane_copy(i, z).start())

        def back():
            loop(1, DEPTH, lambda i: plane_copy(i, lax.rem(z + DEPTH - i, DEPTH)).wait_recv())
            total = planes[0]
            for i in range(1, DEPTH):
                total = total + planes[i]
            gram[piece(chip), :] = total
            loop(1, CHIPS, lambda i: back_copy(i, chip).start())

        def to_pair():
            loop(1, CHIPS, lambda i: back_copy(i, lax.rem(chip + CHIPS - i, CHIPS)).wait_recv())
            pair(1).start()

        def done():
            ref = gram.at[away]
            remote(ref, ref, two_send.at[1], two_recv.at[1], twin_id).wait_recv()
            s_ref[0:deep, p * TILE:p * TILE + W] = gram[0:deep, :]
            s_ref[0:deep, p * TILE + W:(p + 1) * TILE] = gram[deep:, :]

        def sent_there():
            pair(0).wait_send()
            loop(1, CHIPS, lambda i: chip_copy(i).wait_send())
            loop(1, DEPTH, lambda i: plane_copy(i, z).wait_send())

        def sent_back():
            loop(1, CHIPS, lambda i: back_copy(i, chip).wait_send())

        def sent_pair():
            pair(1).wait_send()

        return local, to_chips, to_planes, back, to_pair, done, sent_there, sent_back, sent_pair

    eye = (lax.broadcasted_iota(jnp.int32, (W, W), 0) == lax.broadcasted_iota(jnp.int32, (W, W), 1)).astype(F32)

    def solve(p):
        a, b, e = p * TILE, p * TILE + W, (p + 1) * TILE
        w = yield from factor(jnp.concatenate([s_ref[a:b, a:b], eye], axis=1))
        inv = w[:, W:]
        first = mm(x_ref[:, a:b], inv, ((1,), (1,)))
        out_ref[:, a:b] = first * scale
        u = mm(inv, s_ref[a:b, b:e], ((1,), (0,)))
        s_ref[b:e, b:e] = s_ref[b:e, b:e] - mm(u, u, ((0,), (0,)))
        w = yield from factor(jnp.concatenate([s_ref[b:e, b:e], eye], axis=1))
        inv2 = w[:, W:]
        second = mm(x_ref[:, b:e] - mm(first, u, ((1,), (0,))), inv2, ((1,), (1,)))
        out_ref[:, b:e] = second * scale
        if p == 0:
            x_ref[:, a:b] = first
            x_ref[:, b:e] = second
            u_ref[0:W, 0:W] = inv
            u_ref[0:W, W:] = jnp.zeros_like(inv)
            u_ref[W:, 0:W] = -mm(inv2, mm(u, inv, ((0,), (0,))), ((1,), (0,)))
            u_ref[W:, W:] = inv2

    def couple():
        u = mm(u_ref[...], s_ref[:TILE, TILE:], ((1,), (0,)))
        s_ref[TILE:, TILE:] = s_ref[TILE:, TILE:] - mm(u, u, ((0,), (0,)))
        x_ref[:, TILE:] = x_ref[:, TILE:] - mm(x_ref[:, :TILE], u, ((1,), (0,)))

    def run(*acts):
        for act in acts:
            act[0](*act[1:])

    def ring_sent():
        for p in range(2):
            for h in range(4):
                for a in range(2 if h == 3 else 4):
                    for way in (0, 1):
                        hop(p, a + 2 if h == 3 and way == 1 else a, h, way).wait_send()

    def rows_sent(q):
        for n in range(4):
            pair_copy(q, n).wait_send()
            near_copy(q, n).wait_send()
        for n in range(2):
            far_copy(q, n).wait_send()
        for s in (1, 2, 3):
            last_copy(q, s).wait_send()

    early, late = gram_steps(0), gram_steps(1)

    for a in range(4):
        ring(0, a, 0)
    run((ring, 1, 0, 0), (ring, 1, 1, 0))
    fetch.wait()
    to_scalars.wait()
    run((build, 0), (build, 1), (build, 2), (build, 3))
    for a in range(4):
        run((ring, 0, a, 1), (build, 4 + a))
    run((ring, 1, 2, 0), (ring, 1, 3, 0), (build, 8))
    for a in range(4):
        run((ring, 0, a, 2), (build, 9 + a))
    run((ring, 1, 0, 1), (ring, 1, 1, 1), (build, 13))
    run((ring, 0, 0, 3), (build, 14), (ring, 0, 1, 3), (build, 15))
    run((ring, 1, 2, 1), (ring, 1, 3, 1), (finish, 0))
    for m in range(4):
        other_rows(0, m)
    for m in range(4):
        run((own_rows, 0, m), (ring, 1, m, 2))
    run((stage1, 0), (stage1, 1), (ring, 1, 0, 3), (ring, 1, 1, 3), (stage2, 0), (stage2, 1))
    finish(1)
    for m in range(4):
        other_rows(1, m)
    run((stage3, 0), (stage3, 1))
    for m in range(4):
        own_rows(1, m)
    run((stage1, 2), (stage1, 3))
    run((stage4, 0), (stage4, 1))
    early[0]()
    early[1]()
    run((stage2, 2), (stage2, 3))
    early[2]()
    run((stage3, 2), (stage3, 3))
    run((stage4, 2), (stage4, 3))
    late[0]()
    late[1]()
    early[3]()
    ring_sent()
    early[4]()
    late[2]()
    early[5]()
    for n, _ in enumerate(solve(0)):
        if n == 8:
            late[3]()
    for q in range(NQ):
        rows_sent(q)
    for n in (6, 7, 8):
        early[n]()
    late[6]()
    late[4]()
    late[7]()
    late[5]()
    couple()
    for _ in solve(1):
        pass
    late[8]()


def basis_of(coords, count, tiles, panel, scale):
    dma = pltpu.SemaphoreType.DMA

    def gram_buffers(p):
        deep = TILE * (p + 1)
        size = deep // CHIPS
        return [VMEM((2 * deep, W), F32), VMEM((deep, W), F32), VMEM((CHIPS, size, W), F32),
                VMEM((DEPTH, size, W), F32), VMEM((2 * deep, W), F32)]

    gram_sems = [dma((2,)), dma((2,)), dma((CHIPS,)), dma((CHIPS,)), dma((DEPTH,)), dma((DEPTH,)),
                 dma((CHIPS,)), dma((CHIPS,))]
    return pl.pallas_call(
        lambda *refs: fused_kernel(scale, *refs),
        out_shape=jax.ShapeDtypeStruct((OWN, K), F32),
        in_specs=[
            pl.BlockSpec(memory_space=VMEM),
            pl.BlockSpec(memory_space=SMEM),
            pl.BlockSpec(memory_space=pltpu.HBM),
            pl.BlockSpec(memory_space=pltpu.HBM),
        ],
        out_specs=pl.BlockSpec(memory_space=VMEM),
        scratch_shapes=[
            VMEM((NB * NB, W), jnp.int32),
            SMEM((NB * NB, W), jnp.int32),
            VMEM((SLOTS, TILE, TILE), BF16),
            VMEM((2, 4, TILE, NB * TILE), BF16),
            VMEM((2, NB * TILE, TILE), BF16),
            VMEM((NQ, 2, 4, 4, OWN, W), F32),
            VMEM((NQ, 4, 4, OWN, W), F32),
            VMEM((NQ, 4, 2, OWN, W), F32),
            VMEM((NQ, 2, 2, OWN, W), F32),
            VMEM((NQ, 4, OWN, W), F32),
            VMEM((NQ, 4, OWN, W), F32),
            VMEM((OWN, K), F32),
            VMEM((K, K), F32),
            VMEM((TILE, TILE), F32),
            *gram_buffers(0),
            *gram_buffers(1),
            dma, dma((2,)), dma, dma((2, 2, 4, 4)), dma((2, 2, 4, 4)), dma((NQ, 4)), dma((NQ, 4)), dma((NQ, 4)), dma((NQ, 4)),
            dma((NQ, 2)), dma((NQ, 2)), dma((NQ, 4)), dma((NQ, 4)),
            *gram_sems,
            *gram_sems,
        ],
        compiler_params=pltpu.CompilerParams(
            vmem_limit_bytes=56 * 2**20, collective_id=0, has_side_effects=True),
        name="panel_basis",
    )(coords, count, tiles, panel)


def local(tiles, coords, counts, panel):
    scale = float((NB * TILE * DEPTH) ** 0.5)
    return basis_of(coords[0, 0].T, counts, tiles[0, 0], panel, scale)


def solution(mesh):
    placed = (
        P("row", "col", None, None, None),
        P("row", "col", None, None),
        P("row", "col"),
        P(("row", "col"), None),
    )
    return jax.shard_map(
        local, mesh=mesh, in_specs=placed, out_specs=P(("col", "row"), None), check_vma=False
    )
```

```python
import jax
import jax.numpy as jnp
from jax import lax
from jax.experimental import pallas as pl
from jax.experimental.pallas import tpu as pltpu
from jax.sharding import PartitionSpec as P

F32 = jnp.float32
BF16 = jnp.bfloat16
HI = lax.Precision.HIGHEST
MESH = pl.DeviceIdType.MESH
VMEM = pltpu.VMEM
SMEM = pltpu.SMEM
TILE = 256
NB = 8
K = 512
SLOTS = 48
CHIPS = 16
DEPTH = 8
W = 128
NQ = 4
OWN = 64
PANEL = 16


def mm(a, b, dims):
    return lax.dot_general(a, b, (dims, ((), ())), precision=HI, preferred_element_type=F32)


def split(v):
    hi = v.astype(BF16)
    rest = v - hi.astype(F32)
    mid = rest.astype(BF16)
    return hi, mid, (rest - mid.astype(F32)).astype(BF16)


def stacked(a, b):
    ah, am, al = split(a)
    bh, bm, bl = split(b)
    return lax.dot_general(
        jnp.concatenate([ah, ah, am, am, ah, al], axis=0),
        jnp.concatenate([bh, bm, bh, bm, bl, bh], axis=0),
        (((0,), (0,)), ((), ())),
        preferred_element_type=F32,
    )


def factor(w):
    sub = lax.broadcasted_iota(jnp.int32, (PANEL, W), 0)
    rows = [w[c:c + PANEL, :] for c in range(0, W, PANEL)]
    for k in range(W // PANEL):
        c0 = k * PANEL
        left, right = rows[k][:, :W], rows[k][:, W:]
        cols = [jnp.broadcast_to(left[:, c0 + j:c0 + j + 1], (PANEL, W)) for j in range(PANEL)]
        pivots = jnp.ones((PANEL, W), F32)
        for j in range(PANEL):
            pivot = cols[j][j:j + 1, :]
            f = jnp.where(sub > j, cols[j] * (1.0 / pivot), 0.0)
            for m in range(j + 1, PANEL):
                cols[m] = cols[m] - f * cols[m][j:j + 1, :]
            if j < PANEL - 1:
                left = left - f * left[j:j + 1, :]
                right = right - f * right[j:j + 1, :]
            pivots = jnp.where(sub == j, pivot, pivots)
        norm = lax.rsqrt(pivots)
        left = left * norm
        rows[k] = jnp.concatenate([left, right * norm], axis=1)
        if c0 + PANEL < W:
            t = stacked(left, rows[k])
            for m in range(k + 1, W // PANEL):
                rows[m] = rows[m] - t[m * PANEL:(m + 1) * PANEL, :]
        yield
    return jnp.concatenate(rows, axis=0)


def fused_kernel(scale, coords_ref, count_ref, tiles_hbm, panel_hbm, out_ref, slot_vec, slot_ref, tiles_ref, at_ref, pan, part, twin, near, far, final,
                 last, x_ref, s_ref, u_ref, *rest):
    bufs = (rest[0:5], rest[5:10])
    (slot_sem, panel_sem, tile_sem, ring_send, ring_recv, pair_send, pair_recv, near_send, near_recv, far_send, far_recv,
     last_send, last_recv) = rest[10:23]
    sems = (rest[23:31], rest[31:39])
    row, z = lax.axis_index("row"), lax.axis_index("col")
    core, chip = row % 2, row // 2
    x, y = chip % 4, chip // 4
    other = 1 - core

    def device(yy, xx, cc, zz):
        return ((yy * 4 + xx) * 2 + cc, zz)

    def ring4(v, step):
        return lax.rem(v + step + 4, 4)

    def at_chip(i):
        return (lax.rem(chip + i, CHIPS) * 2 + core, z)

    def at_plane(i):
        return (row, lax.rem(z + i, DEPTH))

    up, down = at_plane(1), at_plane(DEPTH - 1)
    twin_id = device(y, x, other, z)

    def along(axis, step):
        return device(y, ring4(x, step), core, z) if axis == 0 else device(ring4(y, step), x, core, z)

    def hello(device_of):
        def one(i, carry):
            pl.semaphore_signal(barrier, inc=1, device_id=device_of(i), device_id_type=MESH)
            return carry
        return one

    def block_rows(block, start, count):
        return pl.ds(pl.multiple_of(block * TILE + start, 64), count)

    barrier = pltpu.get_barrier_semaphore()
    lax.fori_loop(1, DEPTH, hello(at_plane), 0)
    lax.fori_loop(1, CHIPS, hello(at_chip), 0)
    pl.semaphore_signal(barrier, inc=1, device_id=twin_id, device_id_type=MESH)
    fetch = pltpu.make_async_copy(tiles_hbm, tiles_ref, tile_sem)
    fetch.start()
    own_panel = [pltpu.make_async_copy(panel_hbm.at[:, pl.ds(p * TILE, TILE)], pan.at[p, block_rows(z, 0, TILE)],
                                       panel_sem.at[p]) for p in range(2)]
    for copy in own_panel:
        copy.start()

    position = coords_ref[0:1, :] * NB + coords_ref[1:2, :]
    slot = lax.broadcasted_iota(jnp.int32, (NB * NB, SLOTS), 1)
    match = (position == lax.broadcasted_iota(jnp.int32, (NB * NB, SLOTS), 0)) & (slot < count_ref[0, 0])
    first = jnp.min(jnp.where(match, slot, SLOTS), axis=1, keepdims=True)
    slot_vec[...] = jnp.broadcast_to(first, (NB * NB, W))
    to_scalars = pltpu.make_async_copy(slot_vec, slot_ref, slot_sem)
    to_scalars.start()
    for copy in own_panel:
        copy.wait()
    pl.semaphore_wait(barrier, DEPTH - 1 + CHIPS - 1 + 1)

    def remote(src, dst, send, recv, peer):
        return pltpu.make_async_remote_copy(
            src_ref=src, dst_ref=dst, send_sem=send, recv_sem=recv, device_id=peer, device_id_type=MESH)

    def ring_copy(p, a, h, way, block):
        ref = pan.at[p, block_rows(block, a * 64, 64)]
        return remote(ref, ref, ring_send.at[way, p, a, h], ring_recv.at[way, p, a, h], up if way == 0 else down)

    def hop(p, a, h, way):
        return ring_copy(p, a, h, way, lax.rem(z + (DEPTH - h if way == 0 else h), DEPTH))

    def came(p, a, h, way):
        ring_copy(p, a, h, way, lax.rem(z + (DEPTH - 1 - h if way == 0 else 1 + h), DEPTH)).wait_recv()

    def ring(p, a, h):
        for way in (0, 1):
            piece = a + 2 if h == 3 and way == 1 else a
            if h > 0:
                came(p, piece, h - 1, way)
            hop(p, piece, h, way).start()

    def finish(p):
        for a in (0, 1):
            came(p, a + 2, 2, 0)
            came(p, a, 2, 1)
            came(p, a, 3, 0)
            came(p, a + 2, 3, 1)

    def build(part_of):
        b, first = part_of // 2, part_of % 2 * 4

        def one(i, carry):
            n = slot_ref[b * NB + i, 0]
            tile = tiles_ref[jnp.minimum(n, SLOTS - 1)]
            tile = jnp.where(n < SLOTS, tile, jnp.zeros_like(tile)).T
            for xl in range(2):
                for c in range(2):
                    at = (xl * 2 + c) * 64
                    to = pl.multiple_of((2 * (i % 2) + xl) * 64, 64)
                    at_ref[c, i // 2, pl.ds(to, 64), b * TILE:(b + 1) * TILE] = tile[at:at + 64, :]
            return carry

        lax.fori_loop(first, first + 4, one, 0)

    def pair_copy(q, m):
        if q % 2 == 0:
            src, dst = part.at[q, other, :, m], twin.at[q, :, m]
        else:
            src, dst = part.at[q, other, m], twin.at[q, m]
        return remote(src, dst, pair_send.at[q, m], pair_recv.at[q, m], twin_id)

    def multiply(p, c, m):
        total = jnp.dot(at_ref[c, m], pan[p], preferred_element_type=F32)
        for xx in range(4):
            piece = total[xx * 64:(xx + 1) * 64, :]
            part[2 * p, c, xx, m] = piece[:, :W]
            part[2 * p + 1, c, m, xx] = piece[:, W:]

    def other_rows(p, m):
        multiply(p, other, m)
        pair_copy(2 * p, m).start()
        pair_copy(2 * p + 1, m).start()

    def own_rows(p, m):
        multiply(p, core, m)

    def here(q):
        return x if q % 2 == 0 else y

    def near_copy(q, n):
        step, half = ((2, 0), (1, 2), (2, 2), (-1, 0))[n]
        ref = twin.at[q, ring4(here(q), step), pl.ds(half, 2)]
        return remote(ref, near.at[q, n], near_send.at[q, n], near_recv.at[q, n], along(q % 2, 1 if n < 2 else -1))

    def far_copy(q, n):
        return remote(near.at[q, 2 * n], far.at[q, n], far_send.at[q, n], far_recv.at[q, n], along(q % 2, 1 - 2 * n))

    def last_copy(q, s):
        return remote(final.at[q, ring4(here(q + 1), s)], last.at[q, s], last_send.at[q, s], last_recv.at[q, s],
                      along(1 - q % 2, s))

    def stage1(q):
        for m in range(4):
            pair_copy(q, m).wait_recv()
        twin[q] = twin[q] + part[q, core]
        for n in (0, 2, 1, 3):
            near_copy(q, n).start()

    def stage2(q):
        u = here(q)
        near_copy(q, 0).wait_recv()
        near[q, 0] = near[q, 0] + twin[q, ring4(u, 1), 0:2]
        far_copy(q, 0).start()
        near_copy(q, 2).wait_recv()
        near[q, 2] = near[q, 2] + twin[q, ring4(u, -1), 2:4]
        far_copy(q, 1).start()

    def stage3(q):
        u = here(q)
        near_copy(q, 1).wait_recv()
        near_copy(q, 3).wait_recv()
        far_copy(q, 0).wait_recv()
        final[q, 0:2] = twin[q, u, 0:2] + near[q, 3] + far[q, 0]
        far_copy(q, 1).wait_recv()
        final[q, 2:4] = twin[q, u, 2:4] + near[q, 1] + far[q, 1]
        for s in (1, 2, 3):
            last_copy(q, s).start()

    def stage4(q):
        v = here(q + 1)
        for s in (1, 2, 3):
            last_copy(q, s).wait_recv()
        x_ref[:, q * W:(q + 1) * W] = final[q, v] + last[q, 1] + last[q, 2] + last[q, 3]

    def gram_steps(p):
        mine, half, parts, planes, gram = bufs[p]
        two_send, two_recv, part_send, part_recv, plane_send, plane_recv, back_send, back_recv = sems[p]
        deep = TILE * (p + 1)
        size = deep // CHIPS
        own = pl.ds(pl.multiple_of(core * deep, 8), deep)
        away = pl.ds(pl.multiple_of(other * deep, 8), deep)

        def pair(n):
            src, dst = (mine.at[away], half) if n == 0 else (gram.at[own], gram.at[own])
            return remote(src, dst, two_send.at[n], two_recv.at[n], twin_id)

        def chip_copy(i):
            there = lax.rem(chip + i, CHIPS)
            return remote(half.at[pl.ds(pl.multiple_of(there * size, 8), size)], parts.at[i],
                          part_send.at[i], part_recv.at[i], at_chip(i))

        def plane_copy(i, which):
            ref = planes.at[which]
            return remote(ref, ref, plane_send.at[i], plane_recv.at[i], at_plane(i))

        def piece(n):
            return pl.ds(pl.multiple_of(core * deep + n * size, 8), size)

        def back_copy(i, which):
            ref = gram.at[piece(which)]
            return remote(ref, ref, back_send.at[i], back_recv.at[i], at_chip(i))

        def loop(low, high, act):
            def one(i, carry):
                act(i)
                return carry
            lax.fori_loop(low, high, one, 0)

        def local():
            g = stacked(x_ref[:, :deep], x_ref[:, p * TILE:(p + 1) * TILE])
            mine[0:deep, :] = g[:, :W]
            mine[deep:, :] = g[:, W:]
            pair(0).start()

        def to_chips():
            pair(0).wait_recv()
            half[...] = half[...] + mine[own, :]
            loop(1, CHIPS, lambda i: chip_copy(i).start())

        def to_planes():
            def add(i, total):
                chip_copy(i).wait_recv()
                return total + parts[i]
            planes[z] = lax.fori_loop(1, CHIPS, add, half[pl.ds(pl.multiple_of(chip * size, 8), size), :])
            loop(1, DEPTH, lambda i: plane_copy(i, z).start())

        def back():
            loop(1, DEPTH, lambda i: plane_copy(i, lax.rem(z + DEPTH - i, DEPTH)).wait_recv())
            total = planes[0]
            for i in range(1, DEPTH):
                total = total + planes[i]
            gram[piece(chip), :] = total
            loop(1, CHIPS, lambda i: back_copy(i, chip).start())

        def to_pair():
            loop(1, CHIPS, lambda i: back_copy(i, lax.rem(chip + CHIPS - i, CHIPS)).wait_recv())
            pair(1).start()

        def done():
            ref = gram.at[away]
            remote(ref, ref, two_send.at[1], two_recv.at[1], twin_id).wait_recv()
            s_ref[0:deep, p * TILE:p * TILE + W] = gram[0:deep, :]
            s_ref[0:deep, p * TILE + W:(p + 1) * TILE] = gram[deep:, :]

        def sent_there():
            pair(0).wait_send()
            loop(1, CHIPS, lambda i: chip_copy(i).wait_send())
            loop(1, DEPTH, lambda i: plane_copy(i, z).wait_send())

        def sent_back():
            loop(1, CHIPS, lambda i: back_copy(i, chip).wait_send())

        def sent_pair():
            pair(1).wait_send()

        return local, to_chips, to_planes, back, to_pair, done, sent_there, sent_back, sent_pair

    eye = (lax.broadcasted_iota(jnp.int32, (W, W), 0) == lax.broadcasted_iota(jnp.int32, (W, W), 1)).astype(F32)

    def solve(p):
        a, b, e = p * TILE, p * TILE + W, (p + 1) * TILE
        w = yield from factor(jnp.concatenate([s_ref[a:b, a:b], eye], axis=1))
        inv = w[:, W:]
        first = mm(x_ref[:, a:b], inv, ((1,), (1,)))
        out_ref[:, a:b] = first * scale
        u = mm(inv, s_ref[a:b, b:e], ((1,), (0,)))
        s_ref[b:e, b:e] = s_ref[b:e, b:e] - mm(u, u, ((0,), (0,)))
        w = yield from factor(jnp.concatenate([s_ref[b:e, b:e], eye], axis=1))
        inv2 = w[:, W:]
        second = mm(x_ref[:, b:e] - mm(first, u, ((1,), (0,))), inv2, ((1,), (1,)))
        out_ref[:, b:e] = second * scale
        if p == 0:
            x_ref[:, a:b] = first
            x_ref[:, b:e] = second
            u_ref[0:W, 0:W] = inv
            u_ref[0:W, W:] = jnp.zeros_like(inv)
            u_ref[W:, 0:W] = -mm(inv2, mm(u, inv, ((0,), (0,))), ((1,), (0,)))
            u_ref[W:, W:] = inv2

    def couple():
        u = mm(u_ref[...], s_ref[:TILE, TILE:], ((1,), (0,)))
        s_ref[TILE:, TILE:] = s_ref[TILE:, TILE:] - mm(u, u, ((0,), (0,)))
        x_ref[:, TILE:] = x_ref[:, TILE:] - mm(x_ref[:, :TILE], u, ((1,), (0,)))

    def run(*acts):
        for act in acts:
            act[0](*act[1:])

    def ring_sent():
        for p in range(2):
            for h in range(4):
                for a in range(2 if h == 3 else 4):
                    for way in (0, 1):
                        hop(p, a + 2 if h == 3 and way == 1 else a, h, way).wait_send()

    def rows_sent(q):
        for n in range(4):
            pair_copy(q, n).wait_send()
            near_copy(q, n).wait_send()
        for n in range(2):
            far_copy(q, n).wait_send()
        for s in (1, 2, 3):
            last_copy(q, s).wait_send()

    early, late = gram_steps(0), gram_steps(1)

    for a in range(4):
        ring(0, a, 0)
    ring(1, 0, 0)
    fetch.wait()
    to_scalars.wait()
    run((build, 0), (build, 1), (build, 2), (build, 3))
    for a in range(4):
        run((ring, 0, a, 1), (build, 4 + a))
    run((ring, 1, 1, 0), (build, 8))
    for a in range(4):
        run((ring, 0, a, 2), (build, 9 + a))
    run((ring, 1, 2, 0), (ring, 1, 3, 0), (build, 13))
    run((ring, 0, 0, 3), (build, 14), (ring, 0, 1, 3), (build, 15))
    for a in range(4):
        ring(1, a, 1)
    finish(0)
    for m in range(4):
        other_rows(0, m)
    for m in range(4):
        run((own_rows, 0, m), (ring, 1, m, 2))
    run((stage1, 0), (stage1, 1), (ring, 1, 0, 3), (ring, 1, 1, 3), (stage2, 0), (stage2, 1))
    finish(1)
    for m in range(4):
        other_rows(1, m)
    run((stage3, 0), (stage3, 1))
    for m in range(4):
        own_rows(1, m)
    run((stage1, 2), (stage1, 3))
    run((stage4, 0), (stage4, 1))
    early[0]()
    early[1]()
    run((stage2, 2), (stage2, 3))
    early[2]()
    rows_sent(0)
    rows_sent(1)
    run((stage3, 2), (stage3, 3))
    run((stage4, 2), (stage4, 3))
    late[0]()
    late[1]()
    rows_sent(2)
    rows_sent(3)
    ring_sent()
    early[3]()
    early[4]()
    late[2]()
    early[5]()
    for n, _ in enumerate(solve(0)):
        if n == 8:
            late[3]()
    late[4]()
    for n in (6, 7, 8):
        early[n]()
    late[6]()
    late[7]()
    late[5]()
    couple()
    for _ in solve(1):
        pass
    late[8]()


def basis_of(coords, count, tiles, panel, scale):
    dma = pltpu.SemaphoreType.DMA

    def gram_buffers(p):
        deep = TILE * (p + 1)
        size = deep // CHIPS
        return [VMEM((2 * deep, W), F32), VMEM((deep, W), F32), VMEM((CHIPS, size, W), F32),
                VMEM((DEPTH, size, W), F32), VMEM((2 * deep, W), F32)]

    gram_sems = [dma((2,)), dma((2,)), dma((CHIPS,)), dma((CHIPS,)), dma((DEPTH,)), dma((DEPTH,)),
                 dma((CHIPS,)), dma((CHIPS,))]
    return pl.pallas_call(
        lambda *refs: fused_kernel(scale, *refs),
        out_shape=jax.ShapeDtypeStruct((OWN, K), F32),
        in_specs=[
            pl.BlockSpec(memory_space=VMEM),
            pl.BlockSpec(memory_space=SMEM),
            pl.BlockSpec(memory_space=pltpu.HBM),
            pl.BlockSpec(memory_space=pltpu.HBM),
        ],
        out_specs=pl.BlockSpec(memory_space=VMEM),
        scratch_shapes=[
            VMEM((NB * NB, W), jnp.int32),
            SMEM((NB * NB, W), jnp.int32),
            VMEM((SLOTS, TILE, TILE), BF16),
            VMEM((2, 4, TILE, NB * TILE), BF16),
            VMEM((2, NB * TILE, TILE), BF16),
            VMEM((NQ, 2, 4, 4, OWN, W), F32),
            VMEM((NQ, 4, 4, OWN, W), F32),
            VMEM((NQ, 4, 2, OWN, W), F32),
            VMEM((NQ, 2, 2, OWN, W), F32),
            VMEM((NQ, 4, OWN, W), F32),
            VMEM((NQ, 4, OWN, W), F32),
            VMEM((OWN, K), F32),
            VMEM((K, K), F32),
            VMEM((TILE, TILE), F32),
            *gram_buffers(0),
            *gram_buffers(1),
            dma, dma((2,)), dma, dma((2, 2, 4, 4)), dma((2, 2, 4, 4)), dma((NQ, 4)), dma((NQ, 4)), dma((NQ, 4)), dma((NQ, 4)),
            dma((NQ, 2)), dma((NQ, 2)), dma((NQ, 4)), dma((NQ, 4)),
            *gram_sems,
            *gram_sems,
        ],
        compiler_params=pltpu.CompilerParams(
            vmem_limit_bytes=56 * 2**20, collective_id=0, has_side_effects=True),
        name="panel_basis",
    )(coords, count, tiles, panel)


def local(tiles, coords, counts, panel):
    scale = float((NB * TILE * DEPTH) ** 0.5)
    return basis_of(coords[0, 0].T, counts, tiles[0, 0], panel, scale)


def solution(mesh):
    placed = (
        P("row", "col", None, None, None),
        P("row", "col", None, None),
        P("row", "col"),
        P(("row", "col"), None),
    )
    return jax.shard_map(
        local, mesh=mesh, in_specs=placed, out_specs=P(("col", "row"), None), check_vma=False
    )
```
